128 devices in a mesh: rows: 4 (over x), cols: 32 (over z, y, core).
Axes of the slice: x: 4, y: 4, z: 4, core: 2. Of those that a mesh axis runs over, the one named last changes fastest.
Arguments:
- values: bfloat16 [2, 2048, 262144], P(None, 'rows', 'cols'), may hold values from -0.01171875 to 0.01171875
- block_ids: int32 [2, 4, 32, 64], P(None, 'rows', 'cols'), may hold values from -1 to 1023, as said below
- labels: int32 [2, 2048], P(None, 'rows'), may hold values from 0 to 1
- table: float32 [1024, 128, 128], P('cols'), may hold values from -3 to 3
- table_acc: float32 [1024, 128, 128], P('cols'), may hold values from 1e-05 to 0.001
- lin: float32 [1024, 128], P('cols'), may hold values from -3 to 3
- lin_acc: float32 [1024, 128], P('cols'), may hold values from 1e-05 to 0.001
Outputs:
- new_table: float32 [1024, 128, 128], P('cols')
- new_lin: float32 [1024, 128], P('cols')
- logits: float32 [2, 2048], P(None, 'rows')
The draws below stay inside these ranges and needn't reach their ends.
Inputs may be any that keep to these rules, and one draw needn't show every extreme that they name: `block_ids`: each list holds its active ids first and -1 after them; active ids of one list are distinct; at most 4 active ids of one list lie in one owner range (id // 32); a list has 48 to 64 active ids and some list has 64; in each minibatch one owner range, drawn from the seed, gets exactly 4 ids from every list.
All inputs are finite; a program needn't handle non-finite values.
Results may differ from the reference program's by a relative error of at most 0.0049.
Values may be sent and summed in bfloat16 or wider, within the bound.
A program may use at most 128 MiB of HBM per device.

```python
import math
import jax
import jax.numpy as jnp
from jax import lax

K = 128
BW = 128
MAXB = 64
ITERS = 2
EX = 512
BLK_DEV = 32
CAP = 4
NBLK = 1024
EXAMPLES = 2048
N_ROWS = 4
N_COLS = 32


def one_list(list_key, hot_owner, filled):
    count_key, order_key, base_key, mix_key = jax.random.split(list_key, 4)
    slot_count = N_COLS * CAP
    count = jnp.where(filled, MAXB, jax.random.randint(count_key, (), 3 * MAXB // 4, MAXB + 1))
    order = jax.random.permutation(order_key, slot_count)
    is_hot = order // CAP == hot_owner
    ranking = jnp.where(is_hot, 0, slot_count) + jnp.arange(slot_count)
    chosen = order[jnp.argsort(ranking)][:MAXB]
    owner_of = chosen // CAP
    rank_in = chosen % CAP
    offsets = jax.random.randint(base_key, (N_COLS,), 0, BLK_DEV)
    local = (offsets[owner_of] + rank_in * (BLK_DEV // CAP)) % BLK_DEV
    blocks = owner_of * BLK_DEV + local
    position = jnp.arange(MAXB)
    shuffle = jax.random.permutation(mix_key, MAXB)
    placing = jnp.where(position < count, shuffle, MAXB + position)
    arranged = blocks[jnp.argsort(placing)]
    return jnp.where(position < count, arranged, -1).astype(jnp.int32)


def draw_block_ids(key, part):
    list_total = ITERS * N_ROWS * N_COLS
    hot_key, list_key = jax.random.split(jax.random.fold_in(key, 7))
    hot = jax.random.randint(hot_key, (ITERS,), 0, N_COLS)
    hot_each = jnp.repeat(hot, N_ROWS * N_COLS)
    list_keys = jax.random.split(list_key, list_total)
    filled = jnp.arange(list_total) % (N_ROWS * N_COLS) == 0
    lists = jax.vmap(one_list)(list_keys, hot_each, filled)
    return lists.reshape(ITERS, N_ROWS, N_COLS, MAXB)


def place_ends(drawn, key, smallest, high):
    dims = drawn.shape
    index_at = [jax.random.randint(jax.random.fold_in(key, axis), (), 0, dims[axis]) for axis in range(len(dims))]
    drawn = drawn.at[tuple(index_at)].set(smallest)
    longest = dims.index(max(dims))
    index_at[longest] = (index_at[longest] + 1) % dims[longest]
    return drawn.at[tuple(index_at)].set(high)


def level_of(key, shape, cuts, low, largest):
    loudness = 1.0
    for dim, blocks in cuts:
        heights = jax.random.uniform(jax.random.fold_in(jax.random.fold_in(key, 6), dim), (blocks,), jnp.float32, low / len(cuts), largest / len(cuts))
        loudness = loudness * jnp.repeat(jnp.exp(heights), shape[dim] // blocks).reshape((-1,) + (1,) * (len(shape) - 1 - dim))
    return loudness


def scatter_about(own_key, shape, scale, limit, shards=(), kind=jnp.bfloat16):
    level = level_of(own_key, shape, shards, -0.22, 0.18) if shards else 1.0
    drawn = jax.random.normal(own_key, shape, jnp.float32) * scale * level
    return jnp.minimum(jnp.maximum(drawn, -limit), limit).astype(kind)


def setup_inputs(seed: int = 0) -> dict:
    keys = jax.random.split(jax.random.key(seed), 8)
    return {
        "values": scatter_about(keys[0], (ITERS, EXAMPLES, N_COLS * MAXB * BW), (N_COLS * MAXB * BW) ** -0.5, 0.01171875, ((1, 4), (2, 32))),
        "block_ids": draw_block_ids(jax.random.fold_in(keys[7], 71), 0),
        "labels": place_ends(jax.random.randint(keys[2], (ITERS, EXAMPLES), 0, 2), jax.random.fold_in(keys[2], 1), 0, 1).astype(jnp.int32),
        "table": scatter_about(keys[3], (NBLK, BW, K), 0.5, 3.0, ((0, 32),), jnp.float32),
        "table_acc": jnp.clip(jnp.exp(math.log(0.001) - 4.6051703 * jax.random.uniform(keys[4], (NBLK, BW, K), jnp.float32) ** level_of(keys[4], (NBLK, BW, K), ((0, 32),), -0.2, 0.2)), 9.999999747378752e-06, 0.001),
        "lin": scatter_about(keys[5], (NBLK, BW), 0.5, 3.0, ((0, 32),), jnp.float32),
        "lin_acc": jnp.clip(jnp.exp(math.log(0.001) - 4.6051703 * jax.random.uniform(keys[6], (NBLK, BW), jnp.float32) ** level_of(keys[6], (NBLK, BW), ((0, 32),), -0.2, 0.2)), 9.999999747378752e-06, 0.001),
    }


learn_rate = 0.2

def masked_rows(features, present):
    mask = jnp.repeat(present, BW)
    return jnp.where(mask[None, :], features, jnp.zeros((), jnp.bfloat16))

def pulled(block_list, table, lin):
    present = block_list >= 0
    safe = jnp.where(present, block_list, 0)
    factor_rows = table[safe].astype(jnp.bfloat16).reshape(MAXB * BW, K)
    linear_rows = lin[safe].astype(jnp.bfloat16).reshape(MAXB * BW)
    return (present, factor_rows, linear_rows)

def partials(features, block_list, table, lin):
    present, factor_rows, linear_rows = pulled(block_list, table, lin)
    active = masked_rows(features, present)
    xv_part = jnp.dot(active, factor_rows, preferred_element_type=jnp.float32)
    factor_float = factor_rows.astype(jnp.float32)
    sumsq = lax.optimization_barrier(jnp.sum(factor_float * factor_float, axis=1))
    active_float = active.astype(jnp.float32)
    sq_part = lax.optimization_barrier(jnp.sum(active_float * active_float * sumsq[None, :], axis=1))
    lin_part = jnp.dot(active, linear_rows, preferred_element_type=jnp.float32)
    return (xv_part, sq_part, lin_part)

def gradients(features, block_list, table, lin, slope, weighted):
    present, factor_rows, linear_rows = pulled(block_list, table, lin)
    active = masked_rows(features, present)
    grad_factor = lax.dot_general(active, weighted, (((0,), (0,)), ((), ())), preferred_element_type=jnp.float32)
    active_float = active.astype(jnp.float32)
    weight_sq = lax.optimization_barrier(jnp.sum(active_float * active_float * slope[:, None], axis=0))
    grad_factor = grad_factor - factor_rows.astype(jnp.float32) * weight_sq[:, None]
    grad_linear = lax.optimization_barrier(jnp.sum(active_float * slope[:, None], axis=0))
    return (grad_factor.astype(jnp.bfloat16).reshape(MAXB, BW, K), grad_linear.astype(jnp.bfloat16).reshape(MAXB, BW))

def reference(values, block_ids, labels, table, table_acc, lin, lin_acc):
    total_blocks = table.shape[0]
    logit_list = []
    for step in range(ITERS):
        grouped = values[step].reshape(N_ROWS, EX, N_COLS, MAXB * BW)
        grad_table = jnp.zeros(table.shape, jnp.float32)
        grad_lin = jnp.zeros(lin.shape, jnp.float32)
        row_logits = []
        for group in range(N_ROWS):
            group_values = grouped[group]
            group_ids = block_ids[step, group]

            def column_stats(column):
                features = lax.dynamic_index_in_dim(group_values, column, 1, False)
                block_list = lax.dynamic_index_in_dim(group_ids, column, 0, False)
                return partials(features, block_list, table, lin)
            xv_all, sq_all, lin_all = lax.map(column_stats, jnp.arange(N_COLS))
            xv_sum = lax.optimization_barrier(jnp.sum(xv_all, axis=0))
            logit = lax.optimization_barrier(jnp.sum(lin_all, axis=0)) + 0.5 * (lax.optimization_barrier(jnp.sum(xv_sum * xv_sum, axis=1)) - lax.optimization_barrier(jnp.sum(sq_all, axis=0)))
            label_rows = labels[step, group * EX:(group + 1) * EX].astype(jnp.float32)
            slope = jax.nn.sigmoid(logit) - label_rows
            weighted = (slope[:, None] * xv_sum).astype(jnp.bfloat16)

            def add_column(column, carry):
                gtab, glin = carry
                features = lax.dynamic_index_in_dim(group_values, column, 1, False)
                block_list = lax.dynamic_index_in_dim(group_ids, column, 0, False)
                tile_grad, lin_grad = gradients(features, block_list, table, lin, slope, weighted)
                target = jnp.where(block_list >= 0, block_list, total_blocks)
                gtab = gtab.at[target].add(tile_grad.astype(jnp.float32), mode='drop')
                glin = glin.at[target].add(lin_grad.astype(jnp.float32), mode='drop')
                return (gtab, glin)
            grad_table, grad_lin = lax.fori_loop(0, N_COLS, add_column, (grad_table, grad_lin))
            row_logits.append(logit)
        table_acc = table_acc + grad_table * grad_table
        table = table - learn_rate * grad_table / jnp.sqrt(table_acc)
        lin_acc = lin_acc + grad_lin * grad_lin
        lin = lin - learn_rate * grad_lin / jnp.sqrt(lin_acc)
        logit_list.append(jnp.concatenate(row_logits))
    return (table, lin, jnp.stack(logit_list))
```

```python
import jax
import jax.numpy as jnp
from jax import lax
from jax.experimental import pallas as pl
from jax.experimental.pallas import tpu as pltpu
from jax.sharding import PartitionSpec as P

MESH = pl.DeviceIdType.MESH
learn_rate = 0.2
ROWS, COLS, ZS, YS = 4, 32, 4, 4
PEERS = ROWS * COLS
SLOTS = 4
WIDTH = 128
EX = 512
PART = EX // COLS
BLOCKS = 32
STEPS = 2
F32, BF16, I32 = jnp.float32, jnp.bfloat16, jnp.int32


def nt(a, b):
    return lax.dot_general(a, b, (((1,), (1,)), ((), ())), preferred_element_type=F32)


def nn(a, b):
    return lax.dot_general(a, b, (((1,), (0,)), ((), ())), preferred_element_type=F32)


def iota(shape, dim):
    return lax.broadcasted_iota(I32, shape, dim)


def kernel(
    holder, wanted, label, table, table_acc, lin, lin_acc, values,
    delta_out, lin_out, logit_out,
    v0, v1, asks, ids_v, ids_s, keys, keys8, tab_f, acc_f, lin_f, lacc_f, tab_b, lin_b,
    pull, pull_lin, got, got_lin, stats, xs, xr, ws, wr, swt, gs, gls, rp, rl, dense, lin_part, lin_got, last,
    v_sem, ask_send, ask_recv, ids_sem, pull_send, pull_recv, plin_send, plin_recv, x_send, x_recv, w_send, w_recv,
    push_send, push_recv, glin_send, glin_recv, sum_send, sum_recv, out_send, out_recv,
):
    r, c = lax.axis_index("rows"), lax.axis_index("cols")
    z, y, k = c // 8, (c // 2) % 4, c % 2

    def offsets(d):
        dz = d % 4
        return dz, (d // 8 + dz) % 4, (d // 4) % 2

    def ahead(d):
        dz, dy, dk = offsets(d)
        return ((z + dz) % 4) * 8 + ((y + dy) % 4) * 2 + (k + dk) % 2

    def behind(d):
        dz, dy, dk = offsets(d)
        return ((z + 4 - dz) % 4) * 8 + ((y + 4 - dy) % 4) * 2 + (k + dk) % 2

    def send(src, dst, send_sem, recv_sem, row, col, home):
        @pl.when(home)
        def _():
            pltpu.make_async_copy(src, dst, recv_sem).start()

        @pl.when(jnp.logical_not(home))
        def _():
            pltpu.make_async_remote_copy(
                src_ref=src, dst_ref=dst, send_sem=send_sem, recv_sem=recv_sem,
                device_id=(row, col), device_id_type=MESH,
            ).start()

    def landed(ref, sem):
        pltpu.make_async_copy(ref, ref, sem).wait()

    for t in range(STEPS):
        v = (v0, v1)[t]

        def bring(j, _):
            columns = pl.ds(pl.multiple_of(j * WIDTH, WIDTH), WIDTH)
            pltpu.make_async_copy(values.at[t, :, columns], v.at[j], v_sem.at[t]).start()
            return 0

        lax.fori_loop(0, 64, bring, 0)

    def ask(d, _):
        tr, tc = (r + d // COLS) % ROWS, ahead(d % COLS)
        send(wanted.at[tc], asks.at[r * COLS + c], ask_send, ask_recv, tr, tc, d == 0)
        return 0

    lax.fori_loop(0, PEERS, ask, 0)

    tab_f[...] = table[...]
    acc_f[...] = table_acc[...]
    lin_f[...] = lin[...]
    lacc_f[...] = lin_acc[...]
    tab_b[0] = jnp.zeros((16, 256), BF16)
    tab_b[pl.ds(1, BLOCKS)] = table[...].astype(BF16).reshape(BLOCKS, 16, 256)
    lin_b[0] = jnp.zeros((1, WIDTH), F32)
    lin_b[pl.ds(1, BLOCKS)] = lin[...].reshape(BLOCKS, 1, WIDTH)

    landed(asks, ask_recv)
    ids = jnp.sum(asks[...].reshape(ROWS, COLS, STEPS, WIDTH), axis=1).reshape(ROWS * STEPS, WIDTH)
    ids_v[...] = ids
    to_scalar = pltpu.make_async_copy(ids_v, ids_s, ids_sem)
    to_scalar.start()
    ids_b = ids.astype(F32).astype(BF16)
    for part in range(4):
        lane = iota((WIDTH, 512), 1) + part * 512
        spread = (iota((WIDTH, 512), 0) == lane // 16).astype(F32).astype(BF16)
        found = nn(ids_b, spread).astype(I32)
        keys[:, part * 512 : (part + 1) * 512] = (found - 1) * 16 + iota((8, 512), 1) % 16
    lane = iota((WIDTH, 256), 1)
    spread = ((iota((WIDTH, 256), 0) == (lane // 8) * 4 + lane % 8) & (lane % 8 < 4)).astype(F32).astype(BF16)
    keys8[...] = nn(ids_b, spread).astype(I32) - 1
    to_scalar.wait()
    landed(asks.at[pl.ds(0, PEERS - 1)], ask_send)

    for t in range(STEPS):
        if t > 0:
            landed(pull.at[pl.ds(0, PEERS - 1)], pull_send)
            landed(pull_lin.at[pl.ds(0, COLS - 1)], plin_send)

        def give(d, _):
            tc = ahead(d)
            for q in range(ROWS):
                tr = (r + q) % ROWS
                place = tr * COLS + tc
                for i in range(SLOTS):
                    pull[place, i] = tab_b[ids_s[tr * STEPS + t, tc * SLOTS + i]]
                send(
                    pull.at[place], got.at[t, c, r], pull_send, pull_recv.at[t, d],
                    tr, tc, (d == 0) & (q == 0),
                )
            return 0

        lax.fori_loop(0, COLS, give, 0)

        def give_lin(d, _):
            tc = ahead(d)
            for i in range(SLOTS):
                pull_lin[tc, pl.ds(i, 1)] = lin_b[ids_s[r * STEPS + t, tc * SLOTS + i]]
            pull_lin[tc, pl.ds(4, 4)] = jnp.zeros((4, WIDTH), F32)
            send(pull_lin.at[tc], got_lin.at[t, c], plin_send, plin_recv.at[t], r, tc, d == 0)
            return 0

        lax.fori_loop(0, COLS, give_lin, 0)

        v = (v0, v1)[t]
        landed(v, v_sem.at[t])
        stats[...] = jnp.zeros_like(stats)
        landed(got_lin.at[t], plin_recv.at[t])

        def block_of(o, i):
            return v[holder[t, o * SLOTS + i]]

        def tile_of(o, i):
            quarters = [got[t, o, q, i] for q in range(ROWS)]
            return jnp.concatenate(
                [quarters[q][:, h * WIDTH : (h + 1) * WIDTH] for q in range(ROWS) for h in range(2)], axis=0
            )

        def use(d, _):
            o = behind(d)
            landed(got.at[t, o], pull_recv.at[t, d])
            total = None
            for i in range(SLOTS):
                block = block_of(o, i)
                tile = tile_of(o, i)
                row = got_lin[t, o, pl.ds(i, 1)].astype(BF16).astype(F32)
                lin_rows = jnp.where(iota((WIDTH, WIDTH), 0) == 0, row, 0.0).astype(BF16)
                left = jnp.concatenate([block, block * block], axis=1)
                right = jnp.concatenate(
                    [
                        jnp.concatenate([tile, jnp.zeros((WIDTH, WIDTH), BF16)], axis=1),
                        jnp.concatenate([lin_rows, tile * tile * jnp.asarray(-0.5, BF16)], axis=1),
                    ],
                    axis=0,
                )
                part = nt(left, right)
                total = part if total is None else total + part
            stats[...] += total
            return 0

        lax.fori_loop(0, COLS, use, 0)

        if t > 0:
            landed(xs.at[pl.ds(0, COLS - 1)], x_send)
            landed(wr.at[t, pl.ds(0, COLS - 1)], w_send)
        xs[:, pl.ds(0, PART)] = stats[:, :WIDTH].reshape(COLS, PART, WIDTH)
        rest = jnp.sum(stats[:, WIDTH:], axis=1, keepdims=True)
        spot = iota((EX, WIDTH), 1) == iota((EX, WIDTH), 0) % PART
        rest = jnp.where(spot, rest, 0.0).reshape(COLS, 2, 8, WIDTH)
        xs[:, pl.ds(PART, 8)] = rest[:, 0] + rest[:, 1]

        def give_x(d, _):
            tc = ahead(d)
            send(xs.at[tc], xr.at[t, c], x_send, x_recv.at[t], r, tc, d == 0)
            return 0

        lax.fori_loop(0, COLS, give_x, 0)
        landed(xr.at[t], x_recv.at[t])
        summed = jnp.sum(xr[t], axis=0)
        xv = summed[:PART]
        rest = summed[PART : PART + 8]
        first = jnp.where(iota((8, WIDTH), 1) < 8, rest, 0.0)
        second = jnp.where(iota((8, WIDTH), 1) >= 8, rest, 0.0)
        rest = jnp.sum(jnp.concatenate([first, second], axis=0), axis=1, keepdims=True)
        logit = jnp.broadcast_to(rest + 0.5 * jnp.sum(xv * xv, axis=1, keepdims=True), (PART, WIDTH))
        slope = 1.0 / (1.0 + jnp.exp(-logit)) - label[t]
        weighted = (slope * xv).astype(BF16)

        def low(a):
            return a - a.astype(BF16).astype(F32)

        lane = iota((PART, WIDTH), 1)
        logit_low = low(logit)
        extra = jnp.where(
            lane < 64,
            jnp.where(lane < 32, slope, low(slope)),
            jnp.where(lane < 96, logit, jnp.where(lane < 112, logit_low, low(logit_low))),
        ).astype(BF16)
        ws[:, :WIDTH] = weighted
        ws[:, WIDTH:] = extra

        def give_w(d, _):
            tc = ahead(d)
            send(ws, wr.at[t, c], w_send, w_recv.at[t], r, tc, d == 0)
            return 0

        lax.fori_loop(0, COLS, give_w, 0)
        landed(wr.at[t], w_recv.at[t])
        turned = wr[t].reshape(EX, 2 * WIDTH).astype(F32).T
        swt[...] = turned.astype(BF16)
        logit_out[pl.ds(t, 1)] = turned[192:193] + turned[224:225] + turned[240:241]

        if t > 0:
            landed(gs.at[pl.ds(0, PEERS - 1)], push_send)
            landed(gls.at[pl.ds(0, COLS - 1)], glin_send)

        def grads(d, _):
            o = ahead(d)
            dz, _, _ = offsets(d)
            lins = []
            for i in range(SLOTS):
                block = block_of(o, i)
                right = jnp.concatenate([block, block * block], axis=1)
                res = nn(swt[...], right)
                both = res[WIDTH : WIDTH + 1] + res[WIDTH + 32 : WIDTH + 33]
                lins.append(both[:, :WIDTH])
                tile = res[:WIDTH, :WIDTH] - tile_of(o, i).astype(F32) * both[:, WIDTH:]
                tile = tile.astype(BF16)
                for q in range(ROWS):
                    for h in range(2):
                        at = 32 * q + 16 * h
                        gs[q * COLS + o, i, :, pl.ds(h * WIDTH, WIDTH)] = tile[at : at + 16]
            gls[o] = jnp.concatenate(lins + [jnp.zeros((4, WIDTH), F32)], axis=0)
            send(gls.at[o], rl.at[t, c], glin_send, glin_recv.at[t], r, o, d == 0)
            for dq in range(ROWS):
                q = (r + dq) % ROWS
                send(
                    gs.at[q * COLS + o], rp.at[t, r * COLS + c], push_send, push_recv.at[t, dz * 4 + dq],
                    q, o, (d == 0) & (dq == 0),
                )
            return 0

        lax.fori_loop(0, COLS, grads, 0)

        landed(rl.at[t], glin_recv.at[t])
        keyed = jnp.broadcast_to(keys8[pl.ds(r * STEPS + t, 1)], (BLOCKS, 256))
        onehot = (iota((BLOCKS, 256), 0) == keyed).astype(F32).astype(BF16)
        if t > 0:
            landed(lin_got.at[t, pl.ds(0, ROWS - 1)], sum_send)
        lin_part[...] = nn(onehot, rl[t].reshape(COLS * 8, WIDTH).astype(BF16))
        for dq in range(ROWS):
            q = (r + dq) % ROWS
            send(lin_part, lin_got.at[t, r], sum_send, sum_recv.at[t], q, c, dq == 0)

        dense[...] = jnp.zeros_like(dense)

        def add(n, _):
            dz, dq = n // 4, n % 4
            rs, zs = (r + 4 - dq) % 4, (z + 4 - dz) % 4
            at = rs * COLS + zs * 8
            landed(rp.at[t, pl.ds(at, 8)], push_recv.at[t, n])
            keyed = keys[pl.ds(rs * STEPS + t, 1), pl.ds(pl.multiple_of(zs * 512, 512), 512)]
            onehot = (iota((512, 512), 0) == jnp.broadcast_to(keyed, (512, 512))).astype(F32).astype(BF16)
            dense[...] += nn(onehot, rp[t, pl.ds(at, 8)].reshape(512, 256))
            return 0

        lax.fori_loop(0, 16, add, 0)

        grad = dense[...]
        acc = acc_f[...] + grad * grad
        acc_f[...] = acc
        new = tab_f[...] - learn_rate * grad / jnp.sqrt(acc)
        tab_f[...] = new
        if t < STEPS - 1:
            tab_b[pl.ds(1, BLOCKS)] = new.astype(BF16).reshape(BLOCKS, 16, 256)
        else:
            last[...] = (table[...] - new).astype(BF16)
            for dq in range(ROWS):
                q = (r + dq) % ROWS
                send(last, delta_out.at[r], out_send, out_recv, q, c, dq == 0)

        landed(lin_got.at[t], sum_recv.at[t])
        grad = lin_got[t, 0] + lin_got[t, 1] + lin_got[t, 2] + lin_got[t, 3]
        acc = lacc_f[...] + grad * grad
        lacc_f[...] = acc
        new = lin_f[...] - learn_rate * grad / jnp.sqrt(acc)
        lin_f[...] = new
        lin_b[pl.ds(1, BLOCKS)] = new.reshape(BLOCKS, 1, WIDTH)

    lin_out[...] = lin_f[...]
    landed(pull.at[pl.ds(0, PEERS - 1)], pull_send)
    landed(pull_lin.at[pl.ds(0, COLS - 1)], plin_send)
    landed(xs.at[pl.ds(0, COLS - 1)], x_send)
    landed(wr.at[0, pl.ds(0, COLS - 1)], w_send)
    landed(gs.at[pl.ds(0, PEERS - 1)], push_send)
    landed(gls.at[pl.ds(0, COLS - 1)], glin_send)
    landed(lin_got.at[0, pl.ds(0, ROWS - 1)], sum_send)
    landed(delta_out, out_recv)
    landed(delta_out.at[pl.ds(0, ROWS - 1)], out_send)


def list_slots(lists):
    listed = lists.shape[1]
    present = lists >= 0
    owner = jnp.where(present, lists // BLOCKS, -1)
    before = jnp.arange(listed)[None, :] < jnp.arange(listed)[:, None]
    same = (owner[:, :, None] == owner[:, None, :]) & before[None]
    rank = jnp.sum(same.astype(I32), axis=2)
    slot = jnp.where(present, owner * SLOTS + rank, -1)
    hits = slot[:, :, None] == jnp.arange(COLS * SLOTS)[None, None, :]
    holder = jnp.sum(jnp.where(hits, jnp.arange(listed)[None, :, None], 0), axis=1)
    wanted = jnp.sum(jnp.where(hits, (lists % BLOCKS)[:, :, None] + 1, 0), axis=1)
    return holder, wanted


def local(values, block_ids, labels, table, table_acc, lin, lin_acc):
    r, c = lax.axis_index("rows"), lax.axis_index("cols")
    holder, wanted = list_slots(block_ids[:, 0, 0])
    mine = (jnp.arange(WIDTH) // SLOTS == c)[None, None, :]
    wanted = jnp.tile(wanted.reshape(STEPS, COLS, SLOTS), (1, 1, COLS))
    wanted = jnp.where(mine, wanted, 0).transpose(1, 0, 2)
    label = lax.dynamic_slice_in_dim(labels, c * PART, PART, axis=1).astype(F32)
    label = jnp.broadcast_to(label[:, :, None], (STEPS, PART, WIDTH))

    def quarter(a):
        a = lax.dynamic_slice_in_dim(a, r * 32, 32, axis=2)
        a = a.reshape(BLOCKS, WIDTH, 2, 16).transpose(0, 3, 2, 1)
        return a.reshape(BLOCKS * 16, 256)

    vmem = pl.BlockSpec(memory_space=pltpu.VMEM)
    hbm = pl.BlockSpec(memory_space=pl.ANY)
    dma, V = pltpu.SemaphoreType.DMA, pltpu.VMEM
    delta, new_lin, logits = pl.pallas_call(
        kernel,
        out_shape=(
            jax.ShapeDtypeStruct((ROWS, BLOCKS * 16, 256), BF16),
            jax.ShapeDtypeStruct((BLOCKS, WIDTH), F32),
            jax.ShapeDtypeStruct((STEPS, EX), F32),
        ),
        in_specs=[pl.BlockSpec(memory_space=pltpu.SMEM)] + [vmem] * 6 + [hbm],
        out_specs=(hbm, vmem, vmem),
        scratch_shapes=[
            V((64, EX, WIDTH), BF16),
            V((64, EX, WIDTH), BF16),
            V((PEERS, STEPS, WIDTH), I32),
            V((8, WIDTH), I32),
            pltpu.SMEM((8, WIDTH), I32),
            V((8, 2048), I32),
            V((8, 256), I32),
            V((512, 256), F32),
            V((512, 256), F32),
            V((BLOCKS, WIDTH), F32),
            V((BLOCKS, WIDTH), F32),
            V((BLOCKS + 1, 16, 256), BF16),
            V((BLOCKS + 1, 1, WIDTH), F32),
            V((PEERS, SLOTS, 16, 256), BF16),
            V((COLS, 8, WIDTH), F32),
            V((STEPS, COLS, ROWS, SLOTS, 16, 256), BF16),
            V((STEPS, COLS, 8, WIDTH), F32),
            V((EX, 256), F32),
            V((COLS, 24, WIDTH), F32),
            V((STEPS, COLS, 24, WIDTH), F32),
            V((PART, 256), BF16),
            V((STEPS, COLS, PART, 256), BF16),
            V((256, EX), BF16),
            V((PEERS, SLOTS, 16, 256), BF16),
            V((COLS, 8, WIDTH), F32),
            V((STEPS, PEERS, SLOTS, 16, 256), BF16),
            V((STEPS, COLS, 8, WIDTH), F32),
            V((512, 256), F32),
            V((BLOCKS, WIDTH), F32),
            V((STEPS, ROWS, BLOCKS, WIDTH), F32),
            V((512, 256), BF16),
            dma((STEPS,)),
            dma, dma, dma,
            dma, dma((STEPS, COLS)),
            dma, dma((STEPS,)),
            dma, dma((STEPS,)),
            dma, dma((STEPS,)),
            dma, dma((STEPS, 16)),
            dma, dma((STEPS,)),
            dma, dma((STEPS,)),
            dma, dma,
        ],
        compiler_params=pltpu.CompilerParams(has_side_effects=True, vmem_limit_bytes=60 * 2**20),
    )(holder, wanted, label, quarter(table), quarter(table_acc), lin, lin_acc, values)
    delta = delta.reshape(ROWS, BLOCKS, 16, 2, WIDTH).transpose(1, 4, 0, 3, 2).reshape(table.shape)
    return table - delta.astype(F32), new_lin, logits


def solution(mesh):
    in_specs = (
        P(None, "rows", "cols"),
        P(None, "rows", "cols", None),
        P(None, "rows"),
        P("cols", None, None),
        P("cols", None, None),
        P("cols", None),
        P("cols", None),
    )
    out_specs = (P("cols", None, None), P("cols", None), P(None, "rows"))
    return jax.shard_map(local, mesh=mesh, in_specs=in_specs, out_specs=out_specs, check_vma=False)
```

```python
import jax
import jax.numpy as jnp
from jax import lax
from jax.experimental import pallas as pl
from jax.experimental.pallas import tpu as pltpu
from jax.sharding import PartitionSpec as P

MESH = pl.DeviceIdType.MESH
learn_rate = 0.2
ROWS, COLS, ZS, YS = 4, 32, 4, 4
PEERS = ROWS * COLS
SLOTS = 4
WIDTH = 128
EX = 512
PART = EX // COLS
BLOCKS = 32
STEPS = 2
F32, BF16, I32 = jnp.float32, jnp.bfloat16, jnp.int32


def nt(a, b):
    return lax.dot_general(a, b, (((1,), (1,)), ((), ())), preferred_element_type=F32)


def nn(a, b):
    return lax.dot_general(a, b, (((1,), (0,)), ((), ())), preferred_element_type=F32)


def iota(shape, dim):
    return lax.broadcasted_iota(I32, shape, dim)


def kernel(
    holder, wanted, labels, lin, lin_acc, table, table_acc, values,
    delta_out, lin_out, logit_out,
    v0, v1, tab_n, acc_n, asks, rows_ids, ids_v, ids_s, keys, keys8, tab_f, tab_0, acc_f, lin_f, lacc_f, tab_b, lin_b,
    pull, pull_lin, got, got_lin, stats, xs, xr, ws, wr, swt, gs, gls, rp, rl, dense, lin_part, lin_got, last, back,
    v_sem, tab_sem, acc_sem, ask_send, ask_recv, row_send, row_recv, ids_sem, pull_send, pull_recv, plin_send, plin_recv, x_send, x_recv, w_send, w_recv,
    push_send, push_recv, glin_send, glin_recv, sum_send, sum_recv, out_send, out_recv,
):
    r, c = lax.axis_index("rows"), lax.axis_index("cols")
    z, y, k = c // 8, (c // 2) % 4, c % 2

    def offsets(d):
        dz = d % 4
        return dz, (d // 8 + dz) % 4, (d // 4) % 2

    def ahead(d):
        dz, dy, dk = offsets(d)
        return ((z + dz) % 4) * 8 + ((y + dy) % 4) * 2 + (k + dk) % 2

    def behind(d):
        dz, dy, dk = offsets(d)
        return ((z + 4 - dz) % 4) * 8 + ((y + 4 - dy) % 4) * 2 + (k + dk) % 2

    def send(src, dst, send_sem, recv_sem, row, col, home):
        @pl.when(home)
        def _():
            pltpu.make_async_copy(src, dst, recv_sem).start()

        @pl.when(jnp.logical_not(home))
        def _():
            pltpu.make_async_remote_copy(
                src_ref=src, dst_ref=dst, send_sem=send_sem, recv_sem=recv_sem,
                device_id=(row, col), device_id_type=MESH,
            ).start()

    def landed(ref, sem):
        pltpu.make_async_copy(ref, ref, sem).wait()

    bring_tab = pltpu.make_async_copy(table, tab_n, tab_sem)
    bring_acc = pltpu.make_async_copy(table_acc, acc_n, acc_sem)
    bring_tab.start()
    bring_acc.start()

    def ask(d, _):
        tc = ahead(d)
        send(wanted.at[tc], asks.at[c], ask_send, ask_recv, r, tc, d == 0)
        return 0

    lax.fori_loop(0, COLS, ask, 0)

    for t in range(STEPS):
        v = (v0, v1)[t]

        def bring(j, _):
            columns = pl.ds(pl.multiple_of(j * WIDTH, WIDTH), WIDTH)
            pltpu.make_async_copy(values.at[t, :, columns], v.at[j], v_sem.at[t]).start()
            return 0

        lax.fori_loop(0, 64, bring, 0)

    lin_f[...] = lin[...]
    lacc_f[...] = lin_acc[...]
    tab_b[0] = jnp.zeros((16, 256), BF16)
    lin_b[0] = jnp.zeros((1, WIDTH), F32)
    lin_b[pl.ds(1, BLOCKS)] = lin[...].reshape(BLOCKS, 1, WIDTH)

    def quarter(src, dst):
        pick = (iota((32, WIDTH), 1) == iota((32, WIDTH), 0) + 32 * r).astype(F32).astype(BF16)

        def turn(n, _):
            rest = src[pl.ds(n * 4, 4)].reshape(4 * WIDTH, WIDTH)
            total = None
            for _ in range(3):
                piece = rest.astype(BF16)
                rest = rest - piece.astype(F32)
                part = nt(pick, piece)
                total = part if total is None else total + part
            for i in range(4):
                for h in range(2):
                    dst[pl.ds(pl.multiple_of(n * 64 + i * 16, 16), 16), h * WIDTH : (h + 1) * WIDTH] = total[
                        h * 16 : (h + 1) * 16, i * WIDTH : (i + 1) * WIDTH
                    ]
            return 0

        lax.fori_loop(0, BLOCKS // 4, turn, 0)

    bring_tab.wait()
    quarter(tab_n, tab_0)
    tab_f[...] = tab_0[...]
    tab_b[pl.ds(1, BLOCKS)] = tab_0[...].astype(BF16).reshape(BLOCKS, 16, 256)

    landed(asks, ask_recv)
    rows_ids[r] = jnp.sum(asks[...], axis=0)
    for dq in range(1, ROWS):
        pltpu.make_async_remote_copy(
            src_ref=rows_ids.at[r], dst_ref=rows_ids.at[r], send_sem=row_send, recv_sem=row_recv.at[dq],
            device_id=((r + dq) % ROWS, c), device_id_type=MESH,
        ).start()
    for dq in range(1, ROWS):
        landed(rows_ids.at[(r + 4 - dq) % ROWS], row_recv.at[dq])
    ids = rows_ids[...].reshape(ROWS * STEPS, WIDTH)
    ids_v[...] = ids
    to_scalar = pltpu.make_async_copy(ids_v, ids_s, ids_sem)
    to_scalar.start()
    ids_b = ids.astype(F32).astype(BF16)
    for part in range(4):
        lane = iota((WIDTH, 512), 1) + part * 512
        spread = (iota((WIDTH, 512), 0) == behind(lane // 64) * 4 + (lane // 16) % 4).astype(F32).astype(BF16)
        found = nn(ids_b, spread).astype(I32)
        keys[:, part * 512 : (part + 1) * 512] = (found - 1) * 16 + iota((8, 512), 1) % 16
    lane = iota((WIDTH, 256), 1)
    spread = ((iota((WIDTH, 256), 0) == (lane // 8) * 4 + lane % 8) & (lane % 8 < 4)).astype(F32).astype(BF16)
    keys8[...] = nn(ids_b, spread).astype(I32) - 1
    to_scalar.wait()
    landed(asks.at[pl.ds(0, COLS - 1)], ask_send)
    landed(rows_ids.at[pl.ds(0, ROWS - 1)], row_send)

    for t in range(STEPS):
        if t > 0:
            landed(pull.at[pl.ds(0, PEERS - 1)], pull_send)
            landed(pull_lin.at[pl.ds(0, COLS - 1)], plin_send)

        def give(d, _):
            tc = ahead(d)
            for i in range(SLOTS):
                pull_lin[tc, pl.ds(i, 1)] = lin_b[ids_s[r * STEPS + t, tc * SLOTS + i]]
            pull_lin[tc, pl.ds(4, 4)] = jnp.zeros((4, WIDTH), F32)
            send(pull_lin.at[tc], got_lin.at[t, c], plin_send, plin_recv.at[t, d], r, tc, d == 0)
            for q in range(ROWS):
                tr = (r + q) % ROWS
                place = tr * COLS + tc
                for i in range(SLOTS):
                    pull[place, i] = tab_b[ids_s[tr * STEPS + t, tc * SLOTS + i]]
                send(
                    pull.at[place], got.at[t, c, r], pull_send, pull_recv.at[t, d],
                    tr, tc, (d == 0) & (q == 0),
                )
            return 0

        lax.fori_loop(0, COLS, give, 0)

        v = (v0, v1)[t]
        if t == 0:
            bring_acc.wait()
            quarter(acc_n, acc_f)
        landed(v, v_sem.at[t])
        stats[...] = jnp.zeros_like(stats)

        def block_of(o, i):
            return v[holder[t, o * SLOTS + i]]

        def tile_of(o, i):
            quarters = [got[t, o, q, i] for q in range(ROWS)]
            return jnp.concatenate(
                [quarters[q][:, h * WIDTH : (h + 1) * WIDTH] for q in range(ROWS) for h in range(2)], axis=0
            )

        def use(d, _):
            o = behind(d)
            landed(got_lin.at[t, o], plin_recv.at[t, d])
            landed(got.at[t, o], pull_recv.at[t, d])
            blocks = [block_of(o, i) for i in range(SLOTS)]
            tiles = [tile_of(o, i) for i in range(SLOTS)]
            stats[:, :WIDTH] += nt(jnp.concatenate(blocks, axis=1), jnp.concatenate(tiles, axis=1))
            rest = None
            for i in range(SLOTS):
                block, tile = blocks[i].astype(F32), tiles[i].astype(F32)
                square = -0.5 * jnp.sum(tile * tile, axis=0, keepdims=True)
                row = got_lin[t, o, pl.ds(i, 1)].astype(BF16).astype(F32)
                part = block * (block * square + row)
                rest = part if rest is None else rest + part
            stats[:, WIDTH:] += rest
            return 0

        lax.fori_loop(0, COLS, use, 0)

        if t > 0:
            landed(xs.at[pl.ds(0, COLS - 1)], x_send)
            landed(wr.at[t, pl.ds(0, COLS - 1)], w_send)
        xs[:, pl.ds(0, PART)] = stats[:, :WIDTH].reshape(COLS, PART, WIDTH)
        rest = jnp.sum(stats[:, WIDTH:], axis=1, keepdims=True)
        spot = iota((EX, WIDTH), 1) == iota((EX, WIDTH), 0) % PART
        rest = jnp.where(spot, rest, 0.0).reshape(COLS, 2, 8, WIDTH)
        xs[:, pl.ds(PART, 8)] = rest[:, 0] + rest[:, 1]

        def give_x(d, _):
            tc = ahead(d)
            send(xs.at[tc], xr.at[t, c], x_send, x_recv.at[t], r, tc, d == 0)
            return 0

        lax.fori_loop(0, COLS, give_x, 0)
        landed(xr.at[t], x_recv.at[t])
        summed = jnp.sum(xr[t], axis=0)
        xv = summed[:PART]
        rest = summed[PART : PART + 8]
        first = jnp.where(iota((8, WIDTH), 1) < 8, rest, 0.0)
        second = jnp.where(iota((8, WIDTH), 1) >= 8, rest, 0.0)
        rest = jnp.sum(jnp.concatenate([first, second], axis=0), axis=1, keepdims=True)
        logit = jnp.broadcast_to(rest + 0.5 * jnp.sum(xv * xv, axis=1, keepdims=True), (PART, WIDTH))
        row = labels[pl.ds(t, 1), pl.ds(pl.multiple_of((c // 8) * WIDTH, WIDTH), WIDTH)].astype(F32)
        mine = iota((PART, WIDTH), 1) == iota((PART, WIDTH), 0) + (c % 8) * PART
        label = jnp.sum(jnp.where(mine, row, 0.0), axis=1, keepdims=True)
        slope = 1.0 / (1.0 + jnp.exp(-logit)) - label
        weighted = (slope * xv).astype(BF16)

        def low(a):
            return a - a.astype(BF16).astype(F32)

        lane = iota((PART, WIDTH), 1)
        logit_low = low(logit)
        extra = jnp.where(
            lane < 64,
            jnp.where(lane < 32, slope, low(slope)),
            jnp.where(lane < 96, logit, jnp.where(lane < 112, logit_low, low(logit_low))),
        ).astype(BF16)
        ws[:, :WIDTH] = weighted
        ws[:, WIDTH:] = extra

        def give_w(d, _):
            tc = ahead(d)
            send(ws, wr.at[t, c], w_send, w_recv.at[t], r, tc, d == 0)
            return 0

        lax.fori_loop(0, COLS, give_w, 0)
        landed(wr.at[t], w_recv.at[t])
        turned = wr[t].reshape(EX, 2 * WIDTH).astype(F32).T
        swt[...] = turned.astype(BF16)
        logit_out[pl.ds(t, 1)] = turned[192:193] + turned[224:225] + turned[240:241]

        if t > 0:
            landed(gs.at[pl.ds(0, PEERS - 1)], push_send)
            landed(gls.at[pl.ds(0, COLS - 1)], glin_send)

        def grads(d, _):
            o = ahead(d)
            lins = []
            for i in range(SLOTS):
                block = block_of(o, i)
                right = jnp.concatenate([block, block * block], axis=1)
                res = nn(swt[...], right)
                both = res[WIDTH : WIDTH + 1] + res[WIDTH + 32 : WIDTH + 33]
                lins.append(both[:, :WIDTH])
                tile = res[:WIDTH, :WIDTH] - tile_of(o, i).astype(F32) * both[:, WIDTH:]
                tile = tile.astype(BF16)
                for q in range(ROWS):
                    for h in range(2):
                        at = 32 * q + 16 * h
                        gs[q * COLS + o, i, :, pl.ds(h * WIDTH, WIDTH)] = tile[at : at + 16]
            gls[o] = jnp.concatenate(lins + [jnp.zeros((4, WIDTH), F32)], axis=0)
            send(gls.at[o], rl.at[t, c], glin_send, glin_recv.at[t], r, o, d == 0)
            for dq in range(ROWS):
                q = (r + dq) % ROWS
                send(
                    gs.at[q * COLS + o], rp.at[t, dq * COLS + d], push_send, push_recv.at[t, (d // 4) * 4 + dq],
                    q, o, (d == 0) & (dq == 0),
                )
            return 0

        lax.fori_loop(0, COLS, grads, 0)

        dense[...] = jnp.zeros_like(dense)

        def add(n, _):
            g, dq = n // 4, n % 4
            rs = (r + 4 - dq) % 4
            at = dq * COLS + g * 4
            landed(rp.at[t, pl.ds(at, 4)], push_recv.at[t, n])
            keyed = keys[pl.ds(rs * STEPS + t, 1), pl.ds(pl.multiple_of(g * 256, 256), 256)]
            onehot = (iota((512, 256), 0) == jnp.broadcast_to(keyed, (512, 256))).astype(F32).astype(BF16)
            dense[...] += nn(onehot, rp[t, pl.ds(at, 4)].reshape(256, 256))
            return 0

        lax.fori_loop(0, 28, add, 0)
        landed(rl.at[t], glin_recv.at[t])
        keyed = jnp.broadcast_to(keys8[pl.ds(r * STEPS + t, 1)], (BLOCKS, 256))
        onehot = (iota((BLOCKS, 256), 0) == keyed).astype(F32).astype(BF16)
        if t > 0:
            landed(lin_got.at[t, pl.ds(0, ROWS - 1)], sum_send)
        lin_part[...] = nn(onehot, rl[t].reshape(COLS * 8, WIDTH).astype(BF16))
        for dq in range(ROWS):
            q = (r + dq) % ROWS
            send(lin_part, lin_got.at[t, r], sum_send, sum_recv.at[t], q, c, dq == 0)

        lax.fori_loop(28, 32, add, 0)

        grad = dense[...]
        acc = acc_f[...] + grad * grad
        acc_f[...] = acc
        new = tab_f[...] - learn_rate * grad / jnp.sqrt(acc)
        tab_f[...] = new
        if t < STEPS - 1:
            tab_b[pl.ds(1, BLOCKS)] = new.astype(BF16).reshape(BLOCKS, 16, 256)
        else:
            last[...] = (tab_0[...] - new).astype(BF16)
            for dq in range(ROWS):
                q = (r + dq) % ROWS
                send(last, back.at[r], out_send, out_recv, q, c, dq == 0)

        landed(lin_got.at[t], sum_recv.at[t])
        grad = lin_got[t, 0] + lin_got[t, 1] + lin_got[t, 2] + lin_got[t, 3]
        acc = lacc_f[...] + grad * grad
        lacc_f[...] = acc
        new = lin_f[...] - learn_rate * grad / jnp.sqrt(acc)
        lin_f[...] = new
        lin_b[pl.ds(1, BLOCKS)] = new.reshape(BLOCKS, 1, WIDTH)

    lin_out[...] = lin_f[...]
    landed(pull.at[pl.ds(0, PEERS - 1)], pull_send)
    landed(pull_lin.at[pl.ds(0, COLS - 1)], plin_send)
    landed(xs.at[pl.ds(0, COLS - 1)], x_send)
    landed(wr.at[0, pl.ds(0, COLS - 1)], w_send)
    landed(gs.at[pl.ds(0, PEERS - 1)], push_send)
    landed(gls.at[pl.ds(0, COLS - 1)], glin_send)
    landed(lin_got.at[0, pl.ds(0, ROWS - 1)], sum_send)
    landed(back, out_recv)
    eye = (iota((WIDTH, WIDTH), 0) == iota((WIDTH, WIDTH), 1)).astype(F32).astype(BF16)

    def back_turn(b, _):
        at = pl.ds(pl.multiple_of(b * 16, 16), 16)
        tile = jnp.concatenate(
            [back[q, at, h * WIDTH : (h + 1) * WIDTH] for q in range(ROWS) for h in range(2)], axis=0
        )
        delta_out[b] = nt(eye, tile).astype(BF16)
        return 0

    lax.fori_loop(0, BLOCKS, back_turn, 0)
    landed(back.at[pl.ds(0, ROWS - 1)], out_send)


def list_slots(lists):
    listed = lists.shape[1]
    present = lists >= 0
    owner = jnp.where(present, lists // BLOCKS, -1)
    before = jnp.arange(listed)[None, :] < jnp.arange(listed)[:, None]
    same = (owner[:, :, None] == owner[:, None, :]) & before[None]
    rank = jnp.sum(same.astype(I32), axis=2)
    slot = jnp.where(present, owner * SLOTS + rank, -1)
    hits = slot[:, :, None] == jnp.arange(COLS * SLOTS)[None, None, :]
    holder = jnp.sum(jnp.where(hits, jnp.arange(listed)[None, :, None], 0), axis=1)
    wanted = jnp.sum(jnp.where(hits, (lists % BLOCKS)[:, :, None] + 1, 0), axis=1)
    return holder, wanted


def local(values, block_ids, labels, table, table_acc, lin, lin_acc):
    c = lax.axis_index("cols")
    holder, wanted = list_slots(block_ids[:, 0, 0])
    mine = (jnp.arange(WIDTH) // SLOTS == c)[None, None, :]
    wanted = jnp.tile(wanted.reshape(STEPS, COLS, SLOTS), (1, 1, COLS))
    wanted = jnp.where(mine, wanted, 0).transpose(1, 0, 2)
    vmem = pl.BlockSpec(memory_space=pltpu.VMEM)
    hbm = pl.BlockSpec(memory_space=pl.ANY)
    dma, V = pltpu.SemaphoreType.DMA, pltpu.VMEM
    delta, new_lin, logits = pl.pallas_call(
        kernel,
        out_shape=(
            jax.ShapeDtypeStruct((BLOCKS, WIDTH, WIDTH), BF16),
            jax.ShapeDtypeStruct((BLOCKS, WIDTH), F32),
            jax.ShapeDtypeStruct((STEPS, EX), F32),
        ),
        in_specs=[pl.BlockSpec(memory_space=pltpu.SMEM)] + [vmem] * 4 + [hbm] * 3,
        out_specs=(vmem, vmem, vmem),
        scratch_shapes=[
            V((64, EX, WIDTH), BF16),
            V((64, EX, WIDTH), BF16),
            V((BLOCKS, WIDTH, WIDTH), F32),
            V((BLOCKS, WIDTH, WIDTH), F32),
            V((COLS, STEPS, WIDTH), I32),
            V((ROWS, STEPS, WIDTH), I32),
            V((8, WIDTH), I32),
            pltpu.SMEM((8, WIDTH), I32),
            V((8, 2048), I32),
            V((8, 256), I32),
            V((512, 256), F32),
            V((512, 256), F32),
            V((512, 256), F32),
            V((BLOCKS, WIDTH), F32),
            V((BLOCKS, WIDTH), F32),
            V((BLOCKS + 1, 16, 256), BF16),
            V((BLOCKS + 1, 1, WIDTH), F32),
            V((PEERS, SLOTS, 16, 256), BF16),
            V((COLS, 8, WIDTH), F32),
            V((STEPS, COLS, ROWS, SLOTS, 16, 256), BF16),
            V((STEPS, COLS, 8, WIDTH), F32),
            V((EX, 256), F32),
            V((COLS, 24, WIDTH), F32),
            V((STEPS, COLS, 24, WIDTH), F32),
            V((PART, 256), BF16),
            V((STEPS, COLS, PART, 256), BF16),
            V((256, EX), BF16),
            V((PEERS, SLOTS, 16, 256), BF16),
            V((COLS, 8, WIDTH), F32),
            V((STEPS, PEERS, SLOTS, 16, 256), BF16),
            V((STEPS, COLS, 8, WIDTH), F32),
            V((512, 256), F32),
            V((BLOCKS, WIDTH), F32),
            V((STEPS, ROWS, BLOCKS, WIDTH), F32),
            V((512, 256), BF16),
            V((ROWS, 512, 256), BF16),
            dma((STEPS,)),
            dma, dma,
            dma, dma,
            dma, dma((ROWS,)), dma,
            dma, dma((STEPS, COLS)),
            dma, dma((STEPS, COLS)),
            dma, dma((STEPS,)),
            dma, dma((STEPS,)),
            dma, dma((STEPS, 32)),
            dma, dma((STEPS,)),
            dma, dma((STEPS,)),
            dma, dma,
        ],
        compiler_params=pltpu.CompilerParams(has_side_effects=True, vmem_limit_bytes=60 * 2**20),
    )(holder, wanted, labels, lin, lin_acc, table, table_acc, values)
    return table - delta.astype(F32), new_lin, logits


def solution(mesh):
    in_specs = (
        P(None, "rows", "cols"),
        P(None, "rows", "cols", None),
        P(None, "rows"),
        P("cols", None, None),
        P("cols", None, None),
        P("cols", None),
        P("cols", None),
    )
    out_specs = (P("cols", None, None), P("cols", None), P(None, "rows"))
    return jax.shard_map(local, mesh=mesh, in_specs=in_specs, out_specs=out_specs, check_vma=False)
```

```python
import functools

import jax
import jax.numpy as jnp
from jax import lax
from jax.experimental import pallas as pl
from jax.experimental.pallas import tpu as pltpu
from jax.sharding import PartitionSpec as P

MESH = pl.DeviceIdType.MESH
learn_rate = 0.2
ROWS, COLS, ZS, YS = 4, 32, 4, 4
PEERS = ROWS * COLS
SLOTS = 4
WIDTH = 128
EX = 512
PART = EX // COLS
BLOCKS = 32
STEPS = 2
F32, BF16, I32 = jnp.float32, jnp.bfloat16, jnp.int32


def nt(a, b):
    return lax.dot_general(a, b, (((1,), (1,)), ((), ())), preferred_element_type=F32)


def nn(a, b):
    return lax.dot_general(a, b, (((1,), (0,)), ((), ())), preferred_element_type=F32)


def iota(shape, dim):
    return lax.broadcasted_iota(I32, shape, dim)


def kernel(
    holder, wanted, labels, lin, lin_acc, table, table_acc, values,
    delta_out, lin_out, logit_out,
    v0, v1, tab_n, acc_n, asks, rows_ids, ids_v, ids_s, mine_v, mine_s, keys, tab_all, tab_f, tab_0, acc_f, lin_f, lacc_f, tab_b, lin_b,
    pull, pull_lin, got, got_lin, got_next, pull_next, stats, xs, xr, ws, wr, swt, gs, gls, rp, rl, dense, lin_part, lin_got, last, back,
    v_sem, tab_sem, acc_sem, ask_send, ask_recv, mine_sem, row_send, row_recv, ids_sem, pull_send, next_send, pull_recv, plin_send, plin_recv, x_send, x_recv, w_send, w_recv,
    push_send, push_recv, glin_send, glin_recv, sum_send, sum_recv, out_send, out_recv,
):
    r, c = lax.axis_index("rows"), lax.axis_index("cols")
    z, y, k = c // 8, (c // 2) % 4, c % 2

    def offsets(d):
        dz = d % 4
        return dz, (d // 8 + dz) % 4, (d // 4) % 2

    def ahead(d):
        dz, dy, dk = offsets(d)
        return ((z + dz) % 4) * 8 + ((y + dy) % 4) * 2 + (k + dk) % 2

    def behind(d):
        dz, dy, dk = offsets(d)
        return ((z + 4 - dz) % 4) * 8 + ((y + 4 - dy) % 4) * 2 + (k + dk) % 2

    def send(src, dst, send_sem, recv_sem, row, col, home):
        @pl.when(home)
        def _():
            pltpu.make_async_copy(src, dst, recv_sem).start()

        @pl.when(jnp.logical_not(home))
        def _():
            pltpu.make_async_remote_copy(
                src_ref=src, dst_ref=dst, send_sem=send_sem, recv_sem=recv_sem,
                device_id=(row, col), device_id_type=MESH,
            ).start()

    def landed(ref, sem):
        pltpu.make_async_copy(ref, ref, sem).wait()

    bring_tab = pltpu.make_async_copy(table, tab_n, tab_sem)
    bring_acc = pltpu.make_async_copy(table_acc, acc_n, acc_sem)
    bring_tab.start()
    bring_acc.start()

    def ask(d, _):
        tc = ahead(d)
        send(wanted.at[tc], asks.at[c], ask_send, ask_recv, r, tc, d == 0)
        return 0

    lax.fori_loop(0, COLS, ask, 0)

    for t in range(STEPS):
        v = (v0, v1)[t]

        def bring(j, _):
            columns = pl.ds(pl.multiple_of(j * WIDTH, WIDTH), WIDTH)
            pltpu.make_async_copy(values.at[t, :, columns], v.at[j], v_sem.at[t]).start()
            return 0

        lax.fori_loop(0, 64, bring, 0)

    lin_f[...] = lin[...]
    lacc_f[...] = lin_acc[...]
    for h in range(2):
        tab_b[h, 0] = jnp.zeros((16, WIDTH), BF16)
    lin_b[0] = jnp.zeros((1, WIDTH), F32)
    lin_b[pl.ds(1, BLOCKS)] = lin[...].reshape(BLOCKS, 1, WIDTH)

    def quarter(src, dst):
        pick = (iota((32, WIDTH), 1) == iota((32, WIDTH), 0) + 32 * r).astype(F32).astype(BF16)

        def turn(n, _):
            rest = src[pl.ds(n * 4, 4)].reshape(4 * WIDTH, WIDTH)
            total = None
            for _ in range(3):
                piece = rest.astype(BF16)
                rest = rest - piece.astype(F32)
                part = nt(pick, piece)
                total = part if total is None else total + part
            for i in range(4):
                for h in range(2):
                    dst[pl.ds(pl.multiple_of(n * 64 + i * 16, 16), 16), h * WIDTH : (h + 1) * WIDTH] = total[
                        h * 16 : (h + 1) * 16, i * WIDTH : (i + 1) * WIDTH
                    ]
            return 0

        lax.fori_loop(0, BLOCKS // 4, turn, 0)

    eye = (iota((WIDTH, WIDTH), 0) == iota((WIDTH, WIDTH), 1)).astype(F32).astype(BF16)
    tab_all[0] = jnp.zeros((ROWS, 16, 256), BF16)
    bring_tab.wait()

    def turn_all(n, _):
        tiles = nt(eye, tab_n[pl.ds(n * 4, 4)].reshape(4 * WIDTH, WIDTH).astype(BF16)).astype(BF16)
        for i in range(4):
            for q in range(ROWS):
                for h in range(2):
                    at = 32 * q + 16 * h
                    tab_all[n * 4 + i + 1, q, :, h * WIDTH : (h + 1) * WIDTH] = tiles[
                        at : at + 16, i * WIDTH : (i + 1) * WIDTH
                    ]
        return 0

    lax.fori_loop(0, BLOCKS // 4, turn_all, 0)

    landed(asks, ask_recv)
    own = jnp.sum(asks[...], axis=0)
    mine_v[...] = own
    rows_ids[r] = own
    to_mine = pltpu.make_async_copy(mine_v, mine_s, mine_sem)
    to_mine.start()
    for dq in range(1, ROWS):
        pltpu.make_async_remote_copy(
            src_ref=rows_ids.at[r], dst_ref=rows_ids.at[r], send_sem=row_send, recv_sem=row_recv.at[dq],
            device_id=((r + dq) % ROWS, c), device_id_type=MESH,
        ).start()
    to_mine.wait()

    def half(h):
        return pl.ds(h * WIDTH, WIDTH)

    def give_lin(t, d, tc):
        for i in range(SLOTS):
            pull_lin[tc, pl.ds(i, 1)] = lin_b[mine_s[t, tc * SLOTS + i]]
        send(pull_lin.at[tc], got_lin.at[t, c], plin_send, plin_recv.at[t, d], r, tc, d == 0)

    def give_first(d, _):
        tc = ahead(d)
        give_lin(0, d, tc)
        for i in range(SLOTS):
            at = mine_s[0, tc * SLOTS + i]
            for q in range(ROWS):
                pull[tc * ROWS + q, i] = tab_all[at, q]
        send(pull.at[pl.ds(tc * ROWS, ROWS)], got.at[c], pull_send, pull_recv.at[d], r, tc, d == 0)
        return 0

    def give_next(h, d, _):
        tc = ahead(d)
        if h == 1:
            give_lin(1, d, tc)
        for q in range(ROWS):
            tr = (r + q) % ROWS
            place = tr * COLS + tc
            for i in range(SLOTS):
                pull_next[h, place, i] = tab_b[h, ids_s[tr * STEPS + 1, tc * SLOTS + i]]
            send(
                pull_next.at[h, place], got_next.at[h, c, r], next_send.at[h], pull_recv.at[COLS + h * COLS + d],
                tr, tc, (d == 0) & (q == 0),
            )
        return 0

    for t in range(STEPS):
        if t == 0:
            lax.fori_loop(0, COLS, give_first, 0)

        if t == 0:
            quarter(tab_n, tab_0)
            tab_f[...] = tab_0[...]
            bring_acc.wait()
            quarter(acc_n, acc_f)
            for dq in range(1, ROWS):
                landed(rows_ids.at[(r + 4 - dq) % ROWS], row_recv.at[dq])
            ids = rows_ids[...].reshape(ROWS * STEPS, WIDTH)
            ids_v[...] = ids
            to_scalar = pltpu.make_async_copy(ids_v, ids_s, ids_sem)
            to_scalar.start()
            ids_b = ids.astype(F32).astype(BF16)
            for part in range(4):
                lane = iota((WIDTH, 512), 1) + part * 512
                spread = (iota((WIDTH, 512), 0) == behind(lane // 64) * 4 + (lane // 16) % 4).astype(F32).astype(BF16)
                found = nn(ids_b, spread).astype(I32)
                keys[:, part * 512 : (part + 1) * 512] = (found - 1) * 16 + iota((8, 512), 1) % 16
            to_scalar.wait()
            landed(asks.at[pl.ds(0, COLS - 1)], ask_send)
            landed(rows_ids.at[pl.ds(0, ROWS - 1)], row_send)
        v = (v0, v1)[t]
        landed(v, v_sem.at[t])
        stats[...] = jnp.zeros_like(stats)

        def block_of(o, i):
            return v[holder[t, o * SLOTS + i]]

        def tile_of(o, i):
            if t > 0:
                return jnp.concatenate([got_next[h, o, q, i] for q in range(ROWS) for h in range(2)], axis=0)
            quarters = [got[o, q, i] for q in range(ROWS)]
            return jnp.concatenate(
                [quarters[q][:, h * WIDTH : (h + 1) * WIDTH] for q in range(ROWS) for h in range(2)], axis=0
            )

        def use(d, _):
            o = behind(d)
            landed(got_lin.at[t, o], plin_recv.at[t, d])
            if t == 0:
                landed(got.at[o], pull_recv.at[d])
            else:
                for h in range(2):
                    landed(got_next.at[h, o], pull_recv.at[COLS + h * COLS + d])
            blocks = [block_of(o, i) for i in range(SLOTS)]
            tiles = [tile_of(o, i) for i in range(SLOTS)]
            stats[:, :WIDTH] += nt(jnp.concatenate(blocks, axis=1), jnp.concatenate(tiles, axis=1))
            rest = None
            for i in range(SLOTS):
                block, tile = blocks[i].astype(F32), tiles[i].astype(F32)
                square = -0.5 * jnp.sum(tile * tile, axis=0, keepdims=True)
                row = got_lin[t, o, pl.ds(i, 1)].astype(BF16).astype(F32)
                part = block * (block * square + row)
                rest = part if rest is None else rest + part
            stats[:, WIDTH:] += rest
            return 0

        lax.fori_loop(0, COLS, use, 0)

        if t > 0:
            landed(xs.at[pl.ds(0, COLS - 1)], x_send)
            landed(wr.at[t, pl.ds(0, COLS - 1)], w_send)
        xs[:, pl.ds(0, PART)] = stats[:, :WIDTH].reshape(COLS, PART, WIDTH)
        rest = jnp.sum(stats[:, WIDTH:], axis=1, keepdims=True)
        spot = iota((EX, WIDTH), 1) == iota((EX, WIDTH), 0) % PART
        rest = jnp.where(spot, rest, 0.0).reshape(COLS, 2, 8, WIDTH)
        xs[:, pl.ds(PART, 8)] = rest[:, 0] + rest[:, 1]

        def give_x(d, _):
            tc = ahead(d)
            send(xs.at[tc], xr.at[t, c], x_send, x_recv.at[t], r, tc, d == 0)
            return 0

        lax.fori_loop(0, COLS, give_x, 0)
        landed(xr.at[t], x_recv.at[t])
        summed = jnp.sum(xr[t], axis=0)
        xv = summed[:PART]
        rest = summed[PART : PART + 8]
        first = jnp.where(iota((8, WIDTH), 1) < 8, rest, 0.0)
        second = jnp.where(iota((8, WIDTH), 1) >= 8, rest, 0.0)
        rest = jnp.sum(jnp.concatenate([first, second], axis=0), axis=1, keepdims=True)
        logit = jnp.broadcast_to(rest + 0.5 * jnp.sum(xv * xv, axis=1, keepdims=True), (PART, WIDTH))
        row = labels[pl.ds(t, 1), pl.ds(pl.multiple_of((c // 8) * WIDTH, WIDTH), WIDTH)].astype(F32)
        mine = iota((PART, WIDTH), 1) == iota((PART, WIDTH), 0) + (c % 8) * PART
        label = jnp.sum(jnp.where(mine, row, 0.0), axis=1, keepdims=True)
        slope = 1.0 / (1.0 + jnp.exp(-logit)) - label
        weighted = (slope * xv).astype(BF16)

        def low(a):
            return a - a.astype(BF16).astype(F32)

        lane = iota((PART, WIDTH), 1)
        logit_low = low(logit)
        extra = jnp.where(
            lane < 64,
            jnp.where(lane < 32, slope, low(slope)),
            jnp.where(lane < 96, logit, jnp.where(lane < 112, logit_low, low(logit_low))),
        ).astype(BF16)
        ws[:, :WIDTH] = weighted
        ws[:, WIDTH:] = extra

        def give_w(d, _):
            tc = ahead(d)
            send(ws, wr.at[t, c], w_send, w_recv.at[t], r, tc, d == 0)
            return 0

        lax.fori_loop(0, COLS, give_w, 0)
        landed(wr.at[t], w_recv.at[t])
        turned = wr[t].reshape(EX, 2 * WIDTH).astype(F32).T
        swt[...] = turned.astype(BF16)
        logit_out[pl.ds(t, 1)] = turned[192:193] + turned[224:225] + turned[240:241]

        if t > 0:
            for h in range(2):
                landed(gs.at[h, pl.ds(0, PEERS - 1)], push_send.at[h])
            landed(gls.at[pl.ds(0, COLS - 1)], glin_send)

        def grads(d, _):
            o = ahead(d)
            lins = []
            for i in range(SLOTS):
                block = block_of(o, i)
                right = jnp.concatenate([block, block * block], axis=1)
                res = nn(swt[...], right)
                both = res[WIDTH : WIDTH + 1] + res[WIDTH + 32 : WIDTH + 33]
                lins.append(both[:, :WIDTH])
                tile = res[:WIDTH, :WIDTH] - tile_of(o, i).astype(F32) * both[:, WIDTH:]
                tile = tile.astype(BF16)
                for q in range(ROWS):
                    for h in range(2):
                        at = 32 * q + 16 * h
                        gs[h, q * COLS + o, i] = tile[at : at + 16]
            gls[o] = jnp.concatenate(lins, axis=0)
            send(gls.at[o], rl.at[t, c], glin_send, glin_recv.at[t], r, o, d == 0)
            push(0, d, 0)
            return 0

        def push(h, d, _):
            o = ahead(d)
            for dq in range(ROWS):
                q = (r + dq) % ROWS
                send(
                    gs.at[h, q * COLS + o], rp.at[t, h, dq * COLS + d],
                    push_send.at[h], push_recv.at[t, h * 32 + (d // 4) * 4 + dq], q, o, (d == 0) & (dq == 0),
                )
            return 0

        lax.fori_loop(0, COLS, grads, 0)
        lax.fori_loop(0, COLS, functools.partial(push, 1), 0)

        dense[...] = jnp.zeros_like(dense)

        def add(h, n, _):
            g, dq = n // 4, n % 4
            rs = (r + 4 - dq) % 4
            at = dq * COLS + g * 4
            landed(rp.at[t, h, pl.ds(at, 4)], push_recv.at[t, h * 32 + n])
            keyed = keys[pl.ds(rs * STEPS + t, 1), pl.ds(pl.multiple_of(g * 256, 256), 256)]
            onehot = (iota((512, 256), 0) == jnp.broadcast_to(keyed, (512, 256))).astype(F32).astype(BF16)
            dense[:, half(h)] += nn(onehot, rp[t, h, pl.ds(at, 4)].reshape(256, WIDTH))
            return 0

        def update(h):
            grad = dense[:, half(h)]
            acc = acc_f[:, half(h)] + grad * grad
            acc_f[:, half(h)] = acc
            new = tab_f[:, half(h)] - learn_rate * grad / jnp.sqrt(acc)
            tab_f[:, half(h)] = new
            if t < STEPS - 1:
                tab_b[h, pl.ds(1, BLOCKS)] = new.astype(BF16).reshape(BLOCKS, 16, WIDTH)
                lax.fori_loop(0, COLS, functools.partial(give_next, h), 0)
            else:
                last[h] = (tab_0[:, half(h)] - new).astype(BF16)
                for dq in range(ROWS):
                    q = (r + dq) % ROWS
                    send(last.at[h], back.at[h, r], out_send.at[h], out_recv.at[h], q, c, dq == 0)

        lax.fori_loop(0, 28, functools.partial(add, 0), 0)
        landed(rl.at[t], glin_recv.at[t])
        keyed = jnp.broadcast_to(ids_v[pl.ds(r * STEPS + t, 1)] - 1, (BLOCKS, WIDTH))
        onehot = (iota((BLOCKS, WIDTH), 0) == keyed).astype(F32).astype(BF16)
        if t > 0:
            landed(lin_got.at[t, pl.ds(0, ROWS - 1)], sum_send)
        lin_part[...] = nn(onehot, rl[t].reshape(COLS * SLOTS, WIDTH).astype(BF16))
        for dq in range(ROWS):
            q = (r + dq) % ROWS
            send(lin_part, lin_got.at[t, r], sum_send, sum_recv.at[t], q, c, dq == 0)

        lax.fori_loop(28, 32, functools.partial(add, 0), 0)
        if t < STEPS - 1:
            landed(pull_lin.at[pl.ds(0, COLS - 1)], plin_send)
        update(0)

        landed(lin_got.at[t], sum_recv.at[t])
        grad = lin_got[t, 0] + lin_got[t, 1] + lin_got[t, 2] + lin_got[t, 3]
        acc = lacc_f[...] + grad * grad
        lacc_f[...] = acc
        new = lin_f[...] - learn_rate * grad / jnp.sqrt(acc)
        lin_f[...] = new
        lin_b[pl.ds(1, BLOCKS)] = new.reshape(BLOCKS, 1, WIDTH)

        lax.fori_loop(0, 32, functools.partial(add, 1), 0)
        update(1)

    lin_out[...] = lin_f[...]
    landed(pull.at[pl.ds(0, PEERS - ROWS)], pull_send)
    for h in range(2):
        landed(pull_next.at[h, pl.ds(0, PEERS - 1)], next_send.at[h])
        landed(gs.at[h, pl.ds(0, PEERS - 1)], push_send.at[h])
        landed(back.at[h], out_recv.at[h])
    landed(pull_lin.at[pl.ds(0, COLS - 1)], plin_send)
    landed(xs.at[pl.ds(0, COLS - 1)], x_send)
    landed(wr.at[0, pl.ds(0, COLS - 1)], w_send)
    landed(gls.at[pl.ds(0, COLS - 1)], glin_send)
    landed(lin_got.at[0, pl.ds(0, ROWS - 1)], sum_send)

    def back_turn(b, _):
        at = pl.ds(pl.multiple_of(b * 16, 16), 16)
        tile = jnp.concatenate(
            [back[h, q, at] for q in range(ROWS) for h in range(2)], axis=0
        )
        delta_out[b] = nt(eye, tile).astype(BF16)
        return 0

    lax.fori_loop(0, BLOCKS, back_turn, 0)
    for h in range(2):
        landed(back.at[h, pl.ds(0, ROWS - 1)], out_send.at[h])


def list_slots(lists):
    listed = lists.shape[1]
    present = lists >= 0
    owner = jnp.where(present, lists // BLOCKS, -1)
    before = jnp.arange(listed)[None, :] < jnp.arange(listed)[:, None]
    same = (owner[:, :, None] == owner[:, None, :]) & before[None]
    rank = jnp.sum(same.astype(I32), axis=2)
    slot = jnp.where(present, owner * SLOTS + rank, -1)
    hits = slot[:, :, None] == jnp.arange(COLS * SLOTS)[None, None, :]
    holder = jnp.sum(jnp.where(hits, jnp.arange(listed)[None, :, None], 0), axis=1)
    wanted = jnp.sum(jnp.where(hits, (lists % BLOCKS)[:, :, None] + 1, 0), axis=1)
    return holder, wanted


def local(values, block_ids, labels, table, table_acc, lin, lin_acc):
    c = lax.axis_index("cols")
    holder, wanted = list_slots(block_ids[:, 0, 0])
    mine = (jnp.arange(WIDTH) // SLOTS == c)[None, None, :]
    wanted = jnp.tile(wanted.reshape(STEPS, COLS, SLOTS), (1, 1, COLS))
    wanted = jnp.where(mine, wanted, 0).transpose(1, 0, 2)
    vmem = pl.BlockSpec(memory_space=pltpu.VMEM)
    hbm = pl.BlockSpec(memory_space=pl.ANY)
    dma, V = pltpu.SemaphoreType.DMA, pltpu.VMEM
    delta, new_lin, logits = pl.pallas_call(
        kernel,
        out_shape=(
            jax.ShapeDtypeStruct((BLOCKS, WIDTH, WIDTH), BF16),
            jax.ShapeDtypeStruct((BLOCKS, WIDTH), F32),
            jax.ShapeDtypeStruct((STEPS, EX), F32),
        ),
        in_specs=[pl.BlockSpec(memory_space=pltpu.SMEM)] + [vmem] * 4 + [hbm] * 3,
        out_specs=(vmem, vmem, vmem),
        scratch_shapes=[
            V((64, EX, WIDTH), BF16),
            V((64, EX, WIDTH), BF16),
            V((BLOCKS, WIDTH, WIDTH), F32),
            V((BLOCKS, WIDTH, WIDTH), F32),
            V((COLS, STEPS, WIDTH), I32),
            V((ROWS, STEPS, WIDTH), I32),
            V((8, WIDTH), I32),
            pltpu.SMEM((8, WIDTH), I32),
            V((STEPS, WIDTH), I32),
            pltpu.SMEM((STEPS, WIDTH), I32),
            V((8, 2048), I32),
            V((BLOCKS + 1, ROWS, 16, 256), BF16),
            V((512, 256), F32),
            V((512, 256), F32),
            V((512, 256), F32),
            V((BLOCKS, WIDTH), F32),
            V((BLOCKS, WIDTH), F32),
            V((2, BLOCKS + 1, 16, WIDTH), BF16),
            V((BLOCKS + 1, 1, WIDTH), F32),
            V((PEERS, SLOTS, 16, 256), BF16),
            V((COLS, SLOTS, WIDTH), F32),
            V((COLS, ROWS, SLOTS, 16, 256), BF16),
            V((STEPS, COLS, SLOTS, WIDTH), F32),
            V((2, COLS, ROWS, SLOTS, 16, WIDTH), BF16),
            V((2, PEERS, SLOTS, 16, WIDTH), BF16),
            V((EX, 256), F32),
            V((COLS, 24, WIDTH), F32),
            V((STEPS, COLS, 24, WIDTH), F32),
            V((PART, 256), BF16),
            V((STEPS, COLS, PART, 256), BF16),
            V((256, EX), BF16),
            V((2, PEERS, SLOTS, 16, WIDTH), BF16),
            V((COLS, SLOTS, WIDTH), F32),
            V((STEPS, 2, PEERS, SLOTS, 16, WIDTH), BF16),
            V((STEPS, COLS, SLOTS, WIDTH), F32),
            V((512, 256), F32),
            V((BLOCKS, WIDTH), F32),
            V((STEPS, ROWS, BLOCKS, WIDTH), F32),
            V((2, 512, WIDTH), BF16),
            V((2, ROWS, 512, WIDTH), BF16),
            dma((STEPS,)),
            dma, dma,
            dma, dma,
            dma, dma, dma((ROWS,)), dma,
            dma, dma((2,)), dma((3 * COLS,)),
            dma, dma((STEPS, COLS)),
            dma, dma((STEPS,)),
            dma, dma((STEPS,)),
            dma((2,)), dma((STEPS, 64)),
            dma, dma((STEPS,)),
            dma, dma((STEPS,)),
            dma((2,)), dma((2,)),
        ],
        compiler_params=pltpu.CompilerParams(has_side_effects=True, vmem_limit_bytes=60 * 2**20),
    )(holder, wanted, labels, lin, lin_acc, table, table_acc, values)
    return table - delta.astype(F32), new_lin, logits


def solution(mesh):
    in_specs = (
        P(None, "rows", "cols"),
        P(None, "rows", "cols", None),
        P(None, "rows"),
        P("cols", None, None),
        P("cols", None, None),
        P("cols", None),
        P("cols", None),
    )
    out_specs = (P("cols", None, None), P("cols", None), P(None, "rows"))
    return jax.shard_map(local, mesh=mesh, in_specs=in_specs, out_specs=out_specs, check_vma=False)
```

```python
import functools

import jax
import jax.numpy as jnp
from jax import lax
from jax.experimental import pallas as pl
from jax.experimental.pallas import tpu as pltpu
from jax.sharding import PartitionSpec as P

MESH = pl.DeviceIdType.MESH
learn_rate = 0.2
ROWS, COLS, ZS, YS = 4, 32, 4, 4
PEERS = ROWS * COLS
SLOTS = 4
WIDTH = 128
EX = 512
PART = EX // COLS
BLOCKS = 32
STEPS = 2
F32, BF16, I32 = jnp.float32, jnp.bfloat16, jnp.int32


def nt(a, b):
    return lax.dot_general(a, b, (((1,), (1,)), ((), ())), preferred_element_type=F32)


def nn(a, b):
    return lax.dot_general(a, b, (((1,), (0,)), ((), ())), preferred_element_type=F32)


def iota(shape, dim):
    return lax.broadcasted_iota(I32, shape, dim)


def kernel(
    holder, wanted, labels, lin, lin_acc, table, table_acc, values,
    delta_out, lin_out, logit_out,
    v0, v1, tab_n, acc_n, asks, rows_ids, ids_v, ids_s, mine_v, mine_s, keys, tab_all, tab_f, tab_0, acc_f, lin_f, lacc_f, tab_b, lin_b,
    pull, pull_lin, got, got_lin, got_next, pull_next, stats, xs, xr, ws, wr, swt, gs, gls, rp, rl, dense, lin_part, lin_got, last, back,
    v_sem, tab_sem, acc_sem, ask_send, ask_recv, mine_sem, row_send, row_recv, ids_sem, pull_send, next_send, pull_recv, plin_send, plin_recv, x_send, x_recv, w_send, w_recv,
    push_send, push_recv, glin_send, glin_recv, sum_send, sum_recv, out_send, out_recv,
):
    r, c = lax.axis_index("rows"), lax.axis_index("cols")
    z, y, k = c // 8, (c // 2) % 4, c % 2

    def offsets(d):
        dz = d % 4
        return dz, (d // 8 + dz) % 4, (d // 4) % 2

    def ahead(d):
        dz, dy, dk = offsets(d)
        ez, ey = dz + k * (dy - dz), dy + k * (dz - dy)
        return ((z + ez) % 4) * 8 + ((y + ey) % 4) * 2 + (k + dk) % 2

    def behind(d):
        dz, dy, dk = offsets(d)
        ks = (k + dk) % 2
        ez, ey = dz + ks * (dy - dz), dy + ks * (dz - dy)
        return ((z + 4 - ez) % 4) * 8 + ((y + 4 - ey) % 4) * 2 + ks

    def send(src, dst, send_sem, recv_sem, row, col, home):
        @pl.when(home)
        def _():
            pltpu.make_async_copy(src, dst, recv_sem).start()

        @pl.when(jnp.logical_not(home))
        def _():
            pltpu.make_async_remote_copy(
                src_ref=src, dst_ref=dst, send_sem=send_sem, recv_sem=recv_sem,
                device_id=(row, col), device_id_type=MESH,
            ).start()

    def landed(ref, sem):
        pltpu.make_async_copy(ref, ref, sem).wait()

    bring_tab = pltpu.make_async_copy(table, tab_n, tab_sem)
    bring_acc = pltpu.make_async_copy(table_acc, acc_n, acc_sem)
    bring_tab.start()
    bring_acc.start()

    def ask(d, _):
        tc = ahead(d)
        send(wanted.at[tc], asks.at[c], ask_send, ask_recv, r, tc, d == 0)
        return 0

    lax.fori_loop(0, COLS, ask, 0)

    for t in range(STEPS):
        v = (v0, v1)[t]

        def bring(j, _):
            columns = pl.ds(pl.multiple_of(j * WIDTH, WIDTH), WIDTH)
            pltpu.make_async_copy(values.at[t, :, columns], v.at[j], v_sem.at[t]).start()
            return 0

        lax.fori_loop(0, 64, bring, 0)

    lin_f[...] = lin[...]
    lacc_f[...] = lin_acc[...]
    for h in range(2):
        tab_b[h, 0] = jnp.zeros((16, WIDTH), BF16)
    lin_b[0] = jnp.zeros((1, WIDTH), F32)
    lin_b[pl.ds(1, BLOCKS)] = lin[...].reshape(BLOCKS, 1, WIDTH)

    def quarter(src, dst):
        pick = (iota((32, WIDTH), 1) == iota((32, WIDTH), 0) + 32 * r).astype(F32).astype(BF16)

        def turn(n, _):
            rest = src[pl.ds(n * 4, 4)].reshape(4 * WIDTH, WIDTH)
            total = None
            for _ in range(3):
                piece = rest.astype(BF16)
                rest = rest - piece.astype(F32)
                part = nt(pick, piece)
                total = part if total is None else total + part
            for i in range(4):
                for h in range(2):
                    dst[pl.ds(pl.multiple_of(n * 64 + i * 16, 16), 16), h * WIDTH : (h + 1) * WIDTH] = total[
                        h * 16 : (h + 1) * 16, i * WIDTH : (i + 1) * WIDTH
                    ]
            return 0

        lax.fori_loop(0, BLOCKS // 4, turn, 0)

    eye = (iota((WIDTH, WIDTH), 0) == iota((WIDTH, WIDTH), 1)).astype(F32).astype(BF16)
    tab_all[0] = jnp.zeros((ROWS, 16, 256), BF16)
    bring_tab.wait()

    def turn_all(n, _):
        tiles = nt(eye, tab_n[pl.ds(n * 4, 4)].reshape(4 * WIDTH, WIDTH).astype(BF16)).astype(BF16)
        for i in range(4):
            for q in range(ROWS):
                for h in range(2):
                    at = 32 * q + 16 * h
                    tab_all[n * 4 + i + 1, q, :, h * WIDTH : (h + 1) * WIDTH] = tiles[
                        at : at + 16, i * WIDTH : (i + 1) * WIDTH
                    ]
        return 0

    lax.fori_loop(0, BLOCKS // 4, turn_all, 0)

    landed(asks, ask_recv)
    own = jnp.sum(asks[...], axis=0)
    mine_v[...] = own
    rows_ids[r] = own
    to_mine = pltpu.make_async_copy(mine_v, mine_s, mine_sem)
    to_mine.start()
    for dq in range(1, ROWS):
        pltpu.make_async_remote_copy(
            src_ref=rows_ids.at[r], dst_ref=rows_ids.at[r], send_sem=row_send, recv_sem=row_recv.at[dq],
            device_id=((r + dq) % ROWS, c), device_id_type=MESH,
        ).start()
    to_mine.wait()

    def half(h):
        return pl.ds(h * WIDTH, WIDTH)

    def give_lin(t, d, tc):
        for i in range(SLOTS):
            pull_lin[tc, pl.ds(i, 1)] = lin_b[mine_s[t, tc * SLOTS + i]]
        send(pull_lin.at[tc], got_lin.at[t, c], plin_send, plin_recv.at[t, d], r, tc, d == 0)

    def give_first(d, _):
        tc = ahead(d)
        give_lin(0, d, tc)
        for i in range(SLOTS):
            at = mine_s[0, tc * SLOTS + i]
            for q in range(ROWS):
                pull[tc * ROWS + q, i] = tab_all[at, q]
        send(pull.at[pl.ds(tc * ROWS, ROWS)], got.at[c], pull_send, pull_recv.at[d], r, tc, d == 0)
        return 0

    def give_next(h, d, _):
        tc = ahead(d)
        if h == 1:
            give_lin(1, d, tc)
        for q in range(ROWS):
            tr = (r + q) % ROWS
            place = tr * COLS + tc
            for i in range(SLOTS):
                pull_next[h, place, i] = tab_b[h, ids_s[tr * STEPS + 1, tc * SLOTS + i]]
            send(
                pull_next.at[h, place], got_next.at[h, c, r], next_send.at[h], pull_recv.at[COLS + h * COLS + d],
                tr, tc, (d == 0) & (q == 0),
            )
        return 0

    for t in range(STEPS):
        if t == 0:
            lax.fori_loop(0, COLS, give_first, 0)

        if t == 0:
            quarter(tab_n, tab_0)
            tab_f[...] = tab_0[...]
            bring_acc.wait()
            quarter(acc_n, acc_f)
            for dq in range(1, ROWS):
                landed(rows_ids.at[(r + 4 - dq) % ROWS], row_recv.at[dq])
            ids = rows_ids[...].reshape(ROWS * STEPS, WIDTH)
            ids_v[...] = ids
            to_scalar = pltpu.make_async_copy(ids_v, ids_s, ids_sem)
            to_scalar.start()
            ids_b = ids.astype(F32).astype(BF16)
            for part in range(4):
                lane = iota((WIDTH, 512), 1) + part * 512
                spread = (iota((WIDTH, 512), 0) == behind(lane // 64) * 4 + (lane // 16) % 4).astype(F32).astype(BF16)
                found = nn(ids_b, spread).astype(I32)
                keys[:, part * 512 : (part + 1) * 512] = (found - 1) * 16 + iota((8, 512), 1) % 16
            to_scalar.wait()
            landed(asks.at[pl.ds(0, COLS - 1)], ask_send)
            landed(rows_ids.at[pl.ds(0, ROWS - 1)], row_send)
        v = (v0, v1)[t]
        landed(v, v_sem.at[t])
        stats[...] = jnp.zeros_like(stats)

        def block_of(o, i):
            return v[holder[t, o * SLOTS + i]]

        def tile_of(o, i):
            if t > 0:
                return jnp.concatenate([got_next[h, o, q, i] for q in range(ROWS) for h in range(2)], axis=0)
            quarters = [got[o, q, i] for q in range(ROWS)]
            return jnp.concatenate(
                [quarters[q][:, h * WIDTH : (h + 1) * WIDTH] for q in range(ROWS) for h in range(2)], axis=0
            )

        def use(d, _):
            o = behind(d)
            landed(got_lin.at[t, o], plin_recv.at[t, d])
            if t == 0:
                landed(got.at[o], pull_recv.at[d])
            else:
                for h in range(2):
                    landed(got_next.at[h, o], pull_recv.at[COLS + h * COLS + d])
            blocks = [block_of(o, i) for i in range(SLOTS)]
            tiles = [tile_of(o, i) for i in range(SLOTS)]
            stats[:, :WIDTH] += nt(jnp.concatenate(blocks, axis=1), jnp.concatenate(tiles, axis=1))
            rest = None
            for i in range(SLOTS):
                block, tile = blocks[i].astype(F32), tiles[i].astype(F32)
                square = -0.5 * jnp.sum(tile * tile, axis=0, keepdims=True)
                row = got_lin[t, o, pl.ds(i, 1)].astype(BF16).astype(F32)
                part = block * (block * square + row)
                rest = part if rest is None else rest + part
            stats[:, WIDTH:] += rest
            return 0

        lax.fori_loop(0, COLS, use, 0)

        if t > 0:
            landed(xs.at[pl.ds(0, COLS - 1)], x_send)
            landed(wr.at[t, pl.ds(0, COLS - 1)], w_send)
        xs[:, pl.ds(0, PART)] = stats[:, :WIDTH].reshape(COLS, PART, WIDTH)
        rest = jnp.sum(stats[:, WIDTH:], axis=1, keepdims=True)
        spot = iota((EX, WIDTH), 1) == iota((EX, WIDTH), 0) % PART
        rest = jnp.where(spot, rest, 0.0).reshape(COLS, 2, 8, WIDTH)
        xs[:, pl.ds(PART, 8)] = rest[:, 0] + rest[:, 1]

        def give_x(d, _):
            tc = ahead(d)
            send(xs.at[tc], xr.at[t, c], x_send, x_recv.at[t], r, tc, d == 0)
            return 0

        lax.fori_loop(0, COLS, give_x, 0)
        landed(xr.at[t], x_recv.at[t])
        summed = jnp.sum(xr[t], axis=0)
        xv = summed[:PART]
        rest = summed[PART : PART + 8]
        first = jnp.where(iota((8, WIDTH), 1) < 8, rest, 0.0)
        second = jnp.where(iota((8, WIDTH), 1) >= 8, rest, 0.0)
        rest = jnp.sum(jnp.concatenate([first, second], axis=0), axis=1, keepdims=True)
        logit = jnp.broadcast_to(rest + 0.5 * jnp.sum(xv * xv, axis=1, keepdims=True), (PART, WIDTH))
        row = labels[pl.ds(t, 1), pl.ds(pl.multiple_of((c // 8) * WIDTH, WIDTH), WIDTH)].astype(F32)
        mine = iota((PART, WIDTH), 1) == iota((PART, WIDTH), 0) + (c % 8) * PART
        label = jnp.sum(jnp.where(mine, row, 0.0), axis=1, keepdims=True)
        slope = 1.0 / (1.0 + jnp.exp(-logit)) - label
        weighted = (slope * xv).astype(BF16)

        def low(a):
            return a - a.astype(BF16).astype(F32)

        lane = iota((PART, WIDTH), 1)
        logit_low = low(logit)
        extra = jnp.where(
            lane < 64,
            jnp.where(lane < 32, slope, low(slope)),
            jnp.where(lane < 96, logit, jnp.where(lane < 112, logit_low, low(logit_low))),
        ).astype(BF16)
        ws[:, :WIDTH] = weighted
        ws[:, WIDTH:] = extra

        def give_w(d, _):
            tc = ahead(d)
            send(ws, wr.at[t, c], w_send, w_recv.at[t], r, tc, d == 0)
            return 0

        lax.fori_loop(0, COLS, give_w, 0)
        landed(wr.at[t], w_recv.at[t])
        turned = wr[t].reshape(EX, 2 * WIDTH).astype(F32).T
        swt[...] = turned.astype(BF16)
        logit_out[pl.ds(t, 1)] = turned[192:193] + turned[224:225] + turned[240:241]

        if t > 0:
            for h in range(2):
                landed(gs.at[h, pl.ds(0, PEERS - 1)], push_send.at[h])
            landed(gls.at[pl.ds(0, COLS - 1)], glin_send)

        def grads(d, _):
            o = ahead(d)
            lins = []
            for i in range(SLOTS):
                block = block_of(o, i)
                right = jnp.concatenate([block, block * block], axis=1)
                res = nn(swt[...], right)
                both = res[WIDTH : WIDTH + 1] + res[WIDTH + 32 : WIDTH + 33]
                lins.append(both[:, :WIDTH])
                tile = res[:WIDTH, :WIDTH] - tile_of(o, i).astype(F32) * both[:, WIDTH:]
                tile = tile.astype(BF16)
                for q in range(ROWS):
                    for h in range(2):
                        at = 32 * q + 16 * h
                        gs[h, q * COLS + o, i] = tile[at : at + 16]
            gls[o] = jnp.concatenate(lins, axis=0)
            send(gls.at[o], rl.at[t, c], glin_send, glin_recv.at[t], r, o, d == 0)
            push(0, d, 0)
            return 0

        def push(h, d, _):
            o = ahead(d)
            for dq in range(ROWS):
                q = (r + dq) % ROWS
                send(
                    gs.at[h, q * COLS + o], rp.at[t, h, dq * COLS + d],
                    push_send.at[h], push_recv.at[t, h * 32 + (d // 4) * 4 + dq], q, o, (d == 0) & (dq == 0),
                )
            return 0

        lax.fori_loop(0, COLS, grads, 0)
        lax.fori_loop(0, COLS, functools.partial(push, 1), 0)

        dense[...] = jnp.zeros_like(dense)

        def add(h, n, _):
            g, dq = n // 4, n % 4
            rs = (r + 4 - dq) % 4
            at = dq * COLS + g * 4
            landed(rp.at[t, h, pl.ds(at, 4)], push_recv.at[t, h * 32 + n])
            keyed = keys[pl.ds(rs * STEPS + t, 1), pl.ds(pl.multiple_of(g * 256, 256), 256)]
            onehot = (iota((512, 256), 0) == jnp.broadcast_to(keyed, (512, 256))).astype(F32).astype(BF16)
            dense[:, half(h)] += nn(onehot, rp[t, h, pl.ds(at, 4)].reshape(256, WIDTH))
            return 0

        def update(h):
            grad = dense[:, half(h)]
            acc = acc_f[:, half(h)] + grad * grad
            acc_f[:, half(h)] = acc
            new = tab_f[:, half(h)] - learn_rate * grad / jnp.sqrt(acc)
            tab_f[:, half(h)] = new
            if t < STEPS - 1:
                tab_b[h, pl.ds(1, BLOCKS)] = new.astype(BF16).reshape(BLOCKS, 16, WIDTH)
                lax.fori_loop(0, COLS, functools.partial(give_next, h), 0)
            else:
                last[h] = (tab_0[:, half(h)] - new).astype(BF16)
                for dq in range(ROWS):
                    q = (r + dq) % ROWS
                    send(last.at[h], back.at[h, r], out_send.at[h], out_recv.at[h], q, c, dq == 0)

        lax.fori_loop(0, 28, functools.partial(add, 0), 0)
        landed(rl.at[t], glin_recv.at[t])
        keyed = jnp.broadcast_to(ids_v[pl.ds(r * STEPS + t, 1)] - 1, (BLOCKS, WIDTH))
        onehot = (iota((BLOCKS, WIDTH), 0) == keyed).astype(F32).astype(BF16)
        if t > 0:
            landed(lin_got.at[t, pl.ds(0, ROWS - 1)], sum_send)
        lin_part[...] = nn(onehot, rl[t].reshape(COLS * SLOTS, WIDTH).astype(BF16))
        for dq in range(ROWS):
            q = (r + dq) % ROWS
            send(lin_part, lin_got.at[t, r], sum_send, sum_recv.at[t], q, c, dq == 0)

        lax.fori_loop(28, 32, functools.partial(add, 0), 0)
        if t < STEPS - 1:
            landed(pull_lin.at[pl.ds(0, COLS - 1)], plin_send)
        update(0)

        landed(lin_got.at[t], sum_recv.at[t])
        grad = lin_got[t, 0] + lin_got[t, 1] + lin_got[t, 2] + lin_got[t, 3]
        acc = lacc_f[...] + grad * grad
        lacc_f[...] = acc
        new = lin_f[...] - learn_rate * grad / jnp.sqrt(acc)
        lin_f[...] = new
        lin_b[pl.ds(1, BLOCKS)] = new.reshape(BLOCKS, 1, WIDTH)

        lax.fori_loop(0, 32, functools.partial(add, 1), 0)
        update(1)

    lin_out[...] = lin_f[...]
    landed(pull.at[pl.ds(0, PEERS - ROWS)], pull_send)
    for h in range(2):
        landed(pull_next.at[h, pl.ds(0, PEERS - 1)], next_send.at[h])
        landed(gs.at[h, pl.ds(0, PEERS - 1)], push_send.at[h])
        landed(back.at[h], out_recv.at[h])
    landed(pull_lin.at[pl.ds(0, COLS - 1)], plin_send)
    landed(xs.at[pl.ds(0, COLS - 1)], x_send)
    landed(wr.at[0, pl.ds(0, COLS - 1)], w_send)
    landed(gls.at[pl.ds(0, COLS - 1)], glin_send)
    landed(lin_got.at[0, pl.ds(0, ROWS - 1)], sum_send)

    def back_turn(b, _):
        at = pl.ds(pl.multiple_of(b * 16, 16), 16)
        tile = jnp.concatenate(
            [back[h, q, at] for q in range(ROWS) for h in range(2)], axis=0
        )
        delta_out[b] = nt(eye, tile).astype(BF16)
        return 0

    lax.fori_loop(0, BLOCKS, back_turn, 0)
    for h in range(2):
        landed(back.at[h, pl.ds(0, ROWS - 1)], out_send.at[h])


def list_slots(lists):
    listed = lists.shape[1]
    present = lists >= 0
    owner = jnp.where(present, lists // BLOCKS, -1)
    before = jnp.arange(listed)[None, :] < jnp.arange(listed)[:, None]
    same = (owner[:, :, None] == owner[:, None, :]) & before[None]
    rank = jnp.sum(same.astype(I32), axis=2)
    slot = jnp.where(present, owner * SLOTS + rank, -1)
    hits = slot[:, :, None] == jnp.arange(COLS * SLOTS)[None, None, :]
    holder = jnp.sum(jnp.where(hits, jnp.arange(listed)[None, :, None], 0), axis=1)
    wanted = jnp.sum(jnp.where(hits, (lists % BLOCKS)[:, :, None] + 1, 0), axis=1)
    return holder, wanted


def local(values, block_ids, labels, table, table_acc, lin, lin_acc):
    c = lax.axis_index("cols")
    holder, wanted = list_slots(block_ids[:, 0, 0])
    mine = (jnp.arange(WIDTH) // SLOTS == c)[None, None, :]
    wanted = jnp.tile(wanted.reshape(STEPS, COLS, SLOTS), (1, 1, COLS))
    wanted = jnp.where(mine, wanted, 0).transpose(1, 0, 2)
    vmem = pl.BlockSpec(memory_space=pltpu.VMEM)
    hbm = pl.BlockSpec(memory_space=pl.ANY)
    dma, V = pltpu.SemaphoreType.DMA, pltpu.VMEM
    delta, new_lin, logits = pl.pallas_call(
        kernel,
        out_shape=(
            jax.ShapeDtypeStruct((BLOCKS, WIDTH, WIDTH), BF16),
            jax.ShapeDtypeStruct((BLOCKS, WIDTH), F32),
            jax.ShapeDtypeStruct((STEPS, EX), F32),
        ),
        in_specs=[pl.BlockSpec(memory_space=pltpu.SMEM)] + [vmem] * 4 + [hbm] * 3,
        out_specs=(vmem, vmem, vmem),
        scratch_shapes=[
            V((64, EX, WIDTH), BF16),
            V((64, EX, WIDTH), BF16),
            V((BLOCKS, WIDTH, WIDTH), F32),
            V((BLOCKS, WIDTH, WIDTH), F32),
            V((COLS, STEPS, WIDTH), I32),
            V((ROWS, STEPS, WIDTH), I32),
            V((8, WIDTH), I32),
            pltpu.SMEM((8, WIDTH), I32),
            V((STEPS, WIDTH), I32),
            pltpu.SMEM((STEPS, WIDTH), I32),
            V((8, 2048), I32),
            V((BLOCKS + 1, ROWS, 16, 256), BF16),
            V((512, 256), F32),
            V((512, 256), F32),
            V((512, 256), F32),
            V((BLOCKS, WIDTH), F32),
            V((BLOCKS, WIDTH), F32),
            V((2, BLOCKS + 1, 16, WIDTH), BF16),
            V((BLOCKS + 1, 1, WIDTH), F32),
            V((PEERS, SLOTS, 16, 256), BF16),
            V((COLS, SLOTS, WIDTH), F32),
            V((COLS, ROWS, SLOTS, 16, 256), BF16),
            V((STEPS, COLS, SLOTS, WIDTH), F32),
            V((2, COLS, ROWS, SLOTS, 16, WIDTH), BF16),
            V((2, PEERS, SLOTS, 16, WIDTH), BF16),
            V((EX, 256), F32),
            V((COLS, 24, WIDTH), F32),
            V((STEPS, COLS, 24, WIDTH), F32),
            V((PART, 256), BF16),
            V((STEPS, COLS, PART, 256), BF16),
            V((256, EX), BF16),
            V((2, PEERS, SLOTS, 16, WIDTH), BF16),
            V((COLS, SLOTS, WIDTH), F32),
            V((STEPS, 2, PEERS, SLOTS, 16, WIDTH), BF16),
            V((STEPS, COLS, SLOTS, WIDTH), F32),
            V((512, 256), F32),
            V((BLOCKS, WIDTH), F32),
            V((STEPS, ROWS, BLOCKS, WIDTH), F32),
            V((2, 512, WIDTH), BF16),
            V((2, ROWS, 512, WIDTH), BF16),
            dma((STEPS,)),
            dma, dma,
            dma, dma,
            dma, dma, dma((ROWS,)), dma,
            dma, dma((2,)), dma((3 * COLS,)),
            dma, dma((STEPS, COLS)),
            dma, dma((STEPS,)),
            dma, dma((STEPS,)),
            dma((2,)), dma((STEPS, 64)),
            dma, dma((STEPS,)),
            dma, dma((STEPS,)),
            dma((2,)), dma((2,)),
        ],
        compiler_params=pltpu.CompilerParams(has_side_effects=True, vmem_limit_bytes=60 * 2**20),
    )(holder, wanted, labels, lin, lin_acc, table, table_acc, values)
    return table - delta.astype(F32), new_lin, logits


def solution(mesh):
    in_specs = (
        P(None, "rows", "cols"),
        P(None, "rows", "cols", None),
        P(None, "rows"),
        P("cols", None, None),
        P("cols", None, None),
        P("cols", None),
        P("cols", None),
    )
    out_specs = (P("cols", None, None), P("cols", None), P(None, "rows"))
    return jax.shard_map(local, mesh=mesh, in_specs=in_specs, out_specs=out_specs, check_vma=False)
```

```python
import functools

import jax
import jax.numpy as jnp
from jax import lax
from jax.experimental import pallas as pl
from jax.experimental.pallas import tpu as pltpu
from jax.sharding import PartitionSpec as P

MESH = pl.DeviceIdType.MESH
learn_rate = 0.2
ROWS, COLS, ZS, YS = 4, 32, 4, 4
PEERS = ROWS * COLS
SLOTS = 4
WIDTH = 128
EX = 512
PART = EX // COLS
BLOCKS = 32
STEPS = 2
F32, BF16, I32 = jnp.float32, jnp.bfloat16, jnp.int32


def nt(a, b):
    return lax.dot_general(a, b, (((1,), (1,)), ((), ())), preferred_element_type=F32)


def nn(a, b):
    return lax.dot_general(a, b, (((1,), (0,)), ((), ())), preferred_element_type=F32)


def iota(shape, dim):
    return lax.broadcasted_iota(I32, shape, dim)


def kernel(
    holder, wanted, labels, lin, lin_acc, table, table_acc, values,
    delta_out, lin_out, logit_out,
    v0, v1, tab_n, acc_n, asks, rows_ids, ids_v, ids_s, mine_v, mine_s, keys, tab_all, tab_f, tab_0, acc_f, lin_f, lacc_f, tab_b, lin_b,
    pull, pull_lin, got, got_lin, got_next, pull_next, stats, xs, xr, ws, wr, swt, gs, gls, rp, rl, dense, lin_part, lin_got, last, back,
    v_sem, tab_sem, acc_sem, ask_send, ask_recv, mine_sem, row_send, row_recv, ids_sem, pull_send, next_send, pull_recv, plin_send, plin_recv, x_send, x_recv, w_send, w_recv,
    push_send, push_recv, glin_send, glin_recv, sum_send, sum_recv, out_send, out_recv,
):
    r, c = lax.axis_index("rows"), lax.axis_index("cols")
    z, y, k = c // 8, (c // 2) % 4, c % 2

    def offsets(d):
        dz = d % 4
        return dz, (d // 8 + dz) % 4, (d // 4) % 2

    def ahead(d):
        dz, dy, dk = offsets(d)
        ez, ey = dz + k * (dy - dz), dy + k * (dz - dy)
        return ((z + ez) % 4) * 8 + ((y + ey) % 4) * 2 + (k + dk) % 2

    def behind(d):
        dz, dy, dk = offsets(d)
        ks = (k + dk) % 2
        ez, ey = dz + ks * (dy - dz), dy + ks * (dz - dy)
        return ((z + 4 - ez) % 4) * 8 + ((y + 4 - ey) % 4) * 2 + ks

    def send(src, dst, send_sem, recv_sem, row, col, home):
        @pl.when(home)
        def _():
            pltpu.make_async_copy(src, dst, recv_sem).start()

        @pl.when(jnp.logical_not(home))
        def _():
            pltpu.make_async_remote_copy(
                src_ref=src, dst_ref=dst, send_sem=send_sem, recv_sem=recv_sem,
                device_id=(row, col), device_id_type=MESH,
            ).start()

    def landed(ref, sem):
        pltpu.make_async_copy(ref, ref, sem).wait()

    bring_tab = pltpu.make_async_copy(table, tab_n, tab_sem)
    bring_acc = pltpu.make_async_copy(table_acc, acc_n, acc_sem)
    bring_tab.start()
    bring_acc.start()

    def ask(d, _):
        tc = ahead(d)
        send(wanted.at[tc], asks.at[c], ask_send, ask_recv, r, tc, d == 0)
        return 0

    lax.fori_loop(0, COLS, ask, 0)

    for t in range(STEPS):
        v = (v0, v1)[t]

        def bring(j, _):
            columns = pl.ds(pl.multiple_of(j * WIDTH, WIDTH), WIDTH)
            pltpu.make_async_copy(values.at[t, :, columns], v.at[j], v_sem.at[t]).start()
            return 0

        lax.fori_loop(0, 64, bring, 0)

    lin_f[...] = lin[...]
    lacc_f[...] = lin_acc[...]
    for h in range(2):
        tab_b[h, 0] = jnp.zeros((16, WIDTH), BF16)
    lin_b[0] = jnp.zeros((1, WIDTH), F32)
    lin_b[pl.ds(1, BLOCKS)] = lin[...].reshape(BLOCKS, 1, WIDTH)

    def quarter(src, dst):
        pick = (iota((32, WIDTH), 1) == iota((32, WIDTH), 0) + 32 * r).astype(F32).astype(BF16)

        def turn(n, _):
            rest = src[pl.ds(n * 4, 4)].reshape(4 * WIDTH, WIDTH)
            total = None
            for _ in range(3):
                piece = rest.astype(BF16)
                rest = rest - piece.astype(F32)
                part = nt(pick, piece)
                total = part if total is None else total + part
            for i in range(4):
                for h in range(2):
                    dst[pl.ds(pl.multiple_of(n * 64 + i * 16, 16), 16), h * WIDTH : (h + 1) * WIDTH] = total[
                        h * 16 : (h + 1) * 16, i * WIDTH : (i + 1) * WIDTH
                    ]
            return 0

        lax.fori_loop(0, BLOCKS // 4, turn, 0)

    eye = (iota((WIDTH, WIDTH), 0) == iota((WIDTH, WIDTH), 1)).astype(F32).astype(BF16)
    tab_all[0] = jnp.zeros((ROWS, 16, 256), BF16)
    bring_tab.wait()

    def turn_all(n, _):
        tiles = nt(eye, tab_n[pl.ds(n * 4, 4)].reshape(4 * WIDTH, WIDTH).astype(BF16)).astype(BF16)
        for i in range(4):
            for q in range(ROWS):
                for h in range(2):
                    at = 32 * q + 16 * h
                    tab_all[n * 4 + i + 1, q, :, h * WIDTH : (h + 1) * WIDTH] = tiles[
                        at : at + 16, i * WIDTH : (i + 1) * WIDTH
                    ]
        return 0

    lax.fori_loop(0, BLOCKS // 4, turn_all, 0)

    landed(asks, ask_recv)
    own = jnp.sum(asks[...], axis=0)
    mine_v[...] = own
    rows_ids[r] = own
    to_mine = pltpu.make_async_copy(mine_v, mine_s, mine_sem)
    to_mine.start()
    for dq in range(1, ROWS):
        pltpu.make_async_remote_copy(
            src_ref=rows_ids.at[r], dst_ref=rows_ids.at[r], send_sem=row_send, recv_sem=row_recv.at[dq],
            device_id=((r + dq) % ROWS, c), device_id_type=MESH,
        ).start()
    to_mine.wait()

    def half(h):
        return pl.ds(h * WIDTH, WIDTH)

    def give_lin(t, d, tc):
        for i in range(SLOTS):
            pull_lin[tc, pl.ds(i, 1)] = lin_b[mine_s[t, tc * SLOTS + i]]
        send(pull_lin.at[tc], got_lin.at[t, c], plin_send, plin_recv.at[t, d], r, tc, d == 0)

    def give_first(d, _):
        tc = ahead(d)
        give_lin(0, d, tc)
        for i in range(SLOTS):
            at = mine_s[0, tc * SLOTS + i]
            for q in range(ROWS):
                pull[tc * ROWS + q, i] = tab_all[at, q]
        send(pull.at[pl.ds(tc * ROWS, ROWS)], got.at[c], pull_send, pull_recv.at[d], r, tc, d == 0)
        return 0

    def give_next(h, d, _):
        tc = ahead(d)
        if h == 1:
            give_lin(1, d, tc)
        for q in range(ROWS):
            tr = (r + q) % ROWS
            place = tr * COLS + tc
            for i in range(SLOTS):
                pull_next[h, place, i] = tab_b[h, ids_s[tr * STEPS + 1, tc * SLOTS + i]]
            send(
                pull_next.at[h, place], got_next.at[h, c, r], next_send.at[h], pull_recv.at[COLS + h * COLS + d],
                tr, tc, (d == 0) & (q == 0),
            )
        return 0

    for t in range(STEPS):
        if t == 0:
            lax.fori_loop(0, COLS, give_first, 0)

        if t == 0:
            quarter(tab_n, tab_0)
            tab_f[...] = tab_0[...]
            bring_acc.wait()
            quarter(acc_n, acc_f)
            for dq in range(1, ROWS):
                landed(rows_ids.at[(r + 4 - dq) % ROWS], row_recv.at[dq])
            ids = rows_ids[...].reshape(ROWS * STEPS, WIDTH)
            ids_v[...] = ids
            to_scalar = pltpu.make_async_copy(ids_v, ids_s, ids_sem)
            to_scalar.start()
            ids_b = ids.astype(F32).astype(BF16)
            for part in range(4):
                lane = iota((WIDTH, 512), 1) + part * 512
                spread = (iota((WIDTH, 512), 0) == behind(lane // 64) * 4 + (lane // 16) % 4).astype(F32).astype(BF16)
                found = nn(ids_b, spread).astype(I32)
                keys[:, part * 512 : (part + 1) * 512] = (found - 1) * 16 + iota((8, 512), 1) % 16
            to_scalar.wait()
            landed(asks.at[pl.ds(0, COLS - 1)], ask_send)
            landed(rows_ids.at[pl.ds(0, ROWS - 1)], row_send)
        v = (v0, v1)[t]
        landed(v, v_sem.at[t])
        stats[...] = jnp.zeros_like(stats)

        def block_of(o, i):
            return v[holder[t, o * SLOTS + i]]

        def tile_of(o, i):
            if t > 0:
                return jnp.concatenate([got_next[h, o, q, i] for q in range(ROWS) for h in range(2)], axis=0)
            quarters = [got[o, q, i] for q in range(ROWS)]
            return jnp.concatenate(
                [quarters[q][:, h * WIDTH : (h + 1) * WIDTH] for q in range(ROWS) for h in range(2)], axis=0
            )

        def use(d, _):
            o = behind(d)
            landed(got_lin.at[t, o], plin_recv.at[t, d])
            if t == 0:
                landed(got.at[o], pull_recv.at[d])
            else:
                for h in range(2):
                    landed(got_next.at[h, o], pull_recv.at[COLS + h * COLS + d])
            blocks = [block_of(o, i) for i in range(SLOTS)]
            tiles = [tile_of(o, i) for i in range(SLOTS)]
            stats[:, :WIDTH] += nt(jnp.concatenate(blocks, axis=1), jnp.concatenate(tiles, axis=1))
            rest = None
            for i in range(SLOTS):
                block, tile = blocks[i].astype(F32), tiles[i].astype(F32)
                square = -0.5 * jnp.sum(tile * tile, axis=0, keepdims=True)
                row = got_lin[t, o, pl.ds(i, 1)].astype(BF16).astype(F32)
                part = block * (block * square + row)
                rest = part if rest is None else rest + part
            stats[:, WIDTH:] += rest
            return 0

        lax.fori_loop(0, COLS, use, 0)

        if t > 0:
            landed(xs.at[pl.ds(0, COLS - 1)], x_send)
            landed(wr.at[t, pl.ds(0, COLS - 1)], w_send)
        xs[:, pl.ds(0, PART)] = stats[:, :WIDTH].reshape(COLS, PART, WIDTH)
        rest = jnp.sum(stats[:, WIDTH:], axis=1, keepdims=True)
        spot = iota((EX, WIDTH), 1) == iota((EX, WIDTH), 0) % PART
        rest = jnp.where(spot, rest, 0.0).reshape(COLS, 2, 8, WIDTH)
        xs[:, pl.ds(PART, 8)] = rest[:, 0] + rest[:, 1]

        def give_x(d, _):
            tc = ahead(d)
            send(xs.at[tc], xr.at[t, c], x_send, x_recv.at[t], r, tc, d == 0)
            return 0

        lax.fori_loop(0, COLS, give_x, 0)
        landed(xr.at[t], x_recv.at[t])
        summed = jnp.sum(xr[t], axis=0)
        xv = summed[:PART]
        rest = summed[PART : PART + 8]
        first = jnp.where(iota((8, WIDTH), 1) < 8, rest, 0.0)
        second = jnp.where(iota((8, WIDTH), 1) >= 8, rest, 0.0)
        rest = jnp.sum(jnp.concatenate([first, second], axis=0), axis=1, keepdims=True)
        logit = jnp.broadcast_to(rest + 0.5 * jnp.sum(xv * xv, axis=1, keepdims=True), (PART, WIDTH))
        row = labels[pl.ds(t, 1), pl.ds(pl.multiple_of((c // 8) * WIDTH, WIDTH), WIDTH)].astype(F32)
        mine = iota((PART, WIDTH), 1) == iota((PART, WIDTH), 0) + (c % 8) * PART
        label = jnp.sum(jnp.where(mine, row, 0.0), axis=1, keepdims=True)
        slope = 1.0 / (1.0 + jnp.exp(-logit)) - label
        weighted = (slope * xv).astype(BF16)

        def low(a):
            return a - a.astype(BF16).astype(F32)

        lane = iota((PART, WIDTH), 1)
        logit_low = low(logit)
        extra = jnp.where(
            lane < 64,
            jnp.where(lane < 32, slope, low(slope)),
            jnp.where(lane < 96, logit, jnp.where(lane < 112, logit_low, low(logit_low))),
        ).astype(BF16)
        ws[:, :WIDTH] = weighted
        ws[:, WIDTH:] = extra

        def give_w(d, _):
            tc = ahead(d)
            send(ws, wr.at[t, c], w_send, w_recv.at[t], r, tc, d == 0)
            return 0

        lax.fori_loop(0, COLS, give_w, 0)
        landed(wr.at[t], w_recv.at[t])
        turned = wr[t].reshape(EX, 2 * WIDTH).astype(F32).T
        swt[...] = turned.astype(BF16)
        logit_out[pl.ds(t, 1)] = turned[192:193] + turned[224:225] + turned[240:241]

        if t > 0:
            for h in range(2):
                landed(gs.at[h, pl.ds(0, PEERS - 1)], push_send.at[h])
            landed(gls.at[pl.ds(0, COLS - 1)], glin_send)

        def grads(d, _):
            o = ahead(d)
            lins = []
            for i in range(SLOTS):
                block = block_of(o, i)
                right = jnp.concatenate([block, block * block], axis=1)
                res = nn(swt[...], right)
                both = res[WIDTH : WIDTH + 1] + res[WIDTH + 32 : WIDTH + 33]
                lins.append(both[:, :WIDTH])
                tile = res[:WIDTH, :WIDTH] - tile_of(o, i).astype(F32) * both[:, WIDTH:]
                tile = tile.astype(BF16)
                for q in range(ROWS):
                    for h in range(2):
                        at = 32 * q + 16 * h
                        gs[h, q * COLS + o, i] = tile[at : at + 16]
            gls[o] = jnp.concatenate(lins, axis=0)
            send(gls.at[o], rl.at[t, c], glin_send, glin_recv.at[t], r, o, d == 0)
            push(0, d, 0)
            return 0

        def push(h, d, _):
            o = ahead(d)
            for dq in range(ROWS):
                q = (r + dq) % ROWS
                send(
                    gs.at[h, q * COLS + o], rp.at[t, h, dq * COLS + d],
                    push_send.at[h], push_recv.at[t, h * 32 + (d // 4) * 4 + dq], q, o, (d == 0) & (dq == 0),
                )
            return 0

        lax.fori_loop(0, COLS, grads, 0)
        lax.fori_loop(0, COLS, functools.partial(push, 1), 0)

        dense[...] = jnp.zeros_like(dense)

        def add(h, n, _):
            g, dq = n // 4, n % 4
            rs = (r + 4 - dq) % 4
            at = dq * COLS + g * 4
            landed(rp.at[t, h, pl.ds(at, 4)], push_recv.at[t, h * 32 + n])
            keyed = keys[pl.ds(rs * STEPS + t, 1), pl.ds(pl.multiple_of(g * 256, 256), 256)]
            onehot = (iota((512, 256), 0) == jnp.broadcast_to(keyed, (512, 256))).astype(F32).astype(BF16)
            dense[:, half(h)] += nn(onehot, rp[t, h, pl.ds(at, 4)].reshape(256, WIDTH))
            return 0

        def update(h):
            grad = dense[:, half(h)]
            acc = acc_f[:, half(h)] + grad * grad
            acc_f[:, half(h)] = acc
            new = tab_f[:, half(h)] - learn_rate * grad / jnp.sqrt(acc)
            tab_f[:, half(h)] = new
            if t < STEPS - 1:
                tab_b[h, pl.ds(1, BLOCKS)] = new.astype(BF16).reshape(BLOCKS, 16, WIDTH)
                lax.fori_loop(0, COLS, functools.partial(give_next, h), 0)
            else:
                last[h] = (tab_0[:, half(h)] - new).astype(BF16)
                for dq in range(ROWS):
                    q = (r + dq) % ROWS
                    send(last.at[h], back.at[h, r], out_send.at[h], out_recv.at[h], q, c, dq == 0)

        lax.fori_loop(0, 28, functools.partial(add, 0), 0)
        landed(rl.at[t], glin_recv.at[t])
        keyed = jnp.broadcast_to(ids_v[pl.ds(r * STEPS + t, 1)] - 1, (BLOCKS, WIDTH))
        onehot = (iota((BLOCKS, WIDTH), 0) == keyed).astype(F32).astype(BF16)
        if t > 0:
            landed(lin_got.at[t, pl.ds(0, ROWS - 1)], sum_send)
        lin_part[...] = nn(onehot, rl[t].reshape(COLS * SLOTS, WIDTH).astype(BF16))
        for dq in range(ROWS):
            q = (r + dq) % ROWS
            send(lin_part, lin_got.at[t, r], sum_send, sum_recv.at[t], q, c, dq == 0)

        lax.fori_loop(28, 32, functools.partial(add, 0), 0)
        if t < STEPS - 1:
            landed(pull_lin.at[pl.ds(0, COLS - 1)], plin_send)
        update(0)

        landed(lin_got.at[t], sum_recv.at[t])
        grad = lin_got[t, 0] + lin_got[t, 1] + lin_got[t, 2] + lin_got[t, 3]
        acc = lacc_f[...] + grad * grad
        lacc_f[...] = acc
        new = lin_f[...] - learn_rate * grad / jnp.sqrt(acc)
        lin_f[...] = new
        lin_b[pl.ds(1, BLOCKS)] = new.reshape(BLOCKS, 1, WIDTH)

        lax.fori_loop(0, 32, functools.partial(add, 1), 0)
        update(1)

    lin_out[...] = lin_f[...]
    landed(pull.at[pl.ds(0, PEERS - ROWS)], pull_send)
    for h in range(2):
        landed(pull_next.at[h, pl.ds(0, PEERS - 1)], next_send.at[h])
        landed(gs.at[h, pl.ds(0, PEERS - 1)], push_send.at[h])
        landed(back.at[h], out_recv.at[h])
    landed(pull_lin.at[pl.ds(0, COLS - 1)], plin_send)
    landed(xs.at[pl.ds(0, COLS - 1)], x_send)
    landed(wr.at[0, pl.ds(0, COLS - 1)], w_send)
    landed(gls.at[pl.ds(0, COLS - 1)], glin_send)
    landed(lin_got.at[0, pl.ds(0, ROWS - 1)], sum_send)

    def back_turn(n, _):
        for i in range(8):
            b = n * 8 + i
            at = pl.ds(pl.multiple_of(b * 16, 16), 16)
            tile = jnp.concatenate([back[h, q, at] for q in range(ROWS) for h in range(2)], axis=0)
            delta_out[b] = nt(eye, tile).astype(BF16)
        return 0

    lax.fori_loop(0, BLOCKS // 8, back_turn, 0)
    for h in range(2):
        landed(back.at[h, pl.ds(0, ROWS - 1)], out_send.at[h])


def list_slots(lists):
    listed = lists.shape[1]
    present = lists >= 0
    owner = jnp.where(present, lists // BLOCKS, -1)
    before = jnp.arange(listed)[None, :] < jnp.arange(listed)[:, None]
    same = (owner[:, :, None] == owner[:, None, :]) & before[None]
    rank = jnp.sum(same.astype(I32), axis=2)
    slot = jnp.where(present, owner * SLOTS + rank, -1)
    hits = slot[:, :, None] == jnp.arange(COLS * SLOTS)[None, None, :]
    holder = jnp.sum(jnp.where(hits, jnp.arange(listed)[None, :, None], 0), axis=1)
    wanted = jnp.sum(jnp.where(hits, (lists % BLOCKS)[:, :, None] + 1, 0), axis=1)
    return holder, wanted


def local(values, block_ids, labels, table, table_acc, lin, lin_acc):
    c = lax.axis_index("cols")
    holder, wanted = list_slots(block_ids[:, 0, 0])
    mine = (jnp.arange(WIDTH) // SLOTS == c)[None, None, :]
    wanted = jnp.tile(wanted.reshape(STEPS, COLS, SLOTS), (1, 1, COLS))
    wanted = jnp.where(mine, wanted, 0).transpose(1, 0, 2)
    vmem = pl.BlockSpec(memory_space=pltpu.VMEM)
    hbm = pl.BlockSpec(memory_space=pl.ANY)
    dma, V = pltpu.SemaphoreType.DMA, pltpu.VMEM
    delta, new_lin, logits = pl.pallas_call(
        kernel,
        out_shape=(
            jax.ShapeDtypeStruct((BLOCKS, WIDTH, WIDTH), BF16),
            jax.ShapeDtypeStruct((BLOCKS, WIDTH), F32),
            jax.ShapeDtypeStruct((STEPS, EX), F32),
        ),
        in_specs=[pl.BlockSpec(memory_space=pltpu.SMEM)] + [vmem] * 4 + [hbm] * 3,
        out_specs=(vmem, vmem, vmem),
        scratch_shapes=[
            V((64, EX, WIDTH), BF16),
            V((64, EX, WIDTH), BF16),
            V((BLOCKS, WIDTH, WIDTH), F32),
            V((BLOCKS, WIDTH, WIDTH), F32),
            V((COLS, STEPS, WIDTH), I32),
            V((ROWS, STEPS, WIDTH), I32),
            V((8, WIDTH), I32),
            pltpu.SMEM((8, WIDTH), I32),
            V((STEPS, WIDTH), I32),
            pltpu.SMEM((STEPS, WIDTH), I32),
            V((8, 2048), I32),
            V((BLOCKS + 1, ROWS, 16, 256), BF16),
            V((512, 256), F32),
            V((512, 256), F32),
            V((512, 256), F32),
            V((BLOCKS, WIDTH), F32),
            V((BLOCKS, WIDTH), F32),
            V((2, BLOCKS + 1, 16, WIDTH), BF16),
            V((BLOCKS + 1, 1, WIDTH), F32),
            V((PEERS, SLOTS, 16, 256), BF16),
            V((COLS, SLOTS, WIDTH), F32),
            V((COLS, ROWS, SLOTS, 16, 256), BF16),
            V((STEPS, COLS, SLOTS, WIDTH), F32),
            V((2, COLS, ROWS, SLOTS, 16, WIDTH), BF16),
            V((2, PEERS, SLOTS, 16, WIDTH), BF16),
            V((EX, 256), F32),
            V((COLS, 24, WIDTH), F32),
            V((STEPS, COLS, 24, WIDTH), F32),
            V((PART, 256), BF16),
            V((STEPS, COLS, PART, 256), BF16),
            V((256, EX), BF16),
            V((2, PEERS, SLOTS, 16, WIDTH), BF16),
            V((COLS, SLOTS, WIDTH), F32),
            V((STEPS, 2, PEERS, SLOTS, 16, WIDTH), BF16),
            V((STEPS, COLS, SLOTS, WIDTH), F32),
            V((512, 256), F32),
            V((BLOCKS, WIDTH), F32),
            V((STEPS, ROWS, BLOCKS, WIDTH), F32),
            V((2, 512, WIDTH), BF16),
            V((2, ROWS, 512, WIDTH), BF16),
            dma((STEPS,)),
            dma, dma,
            dma, dma,
            dma, dma, dma((ROWS,)), dma,
            dma, dma((2,)), dma((3 * COLS,)),
            dma, dma((STEPS, COLS)),
            dma, dma((STEPS,)),
            dma, dma((STEPS,)),
            dma((2,)), dma((STEPS, 64)),
            dma, dma((STEPS,)),
            dma, dma((STEPS,)),
            dma((2,)), dma((2,)),
        ],
        compiler_params=pltpu.CompilerParams(has_side_effects=True, vmem_limit_bytes=60 * 2**20),
    )(holder, wanted, labels, lin, lin_acc, table, table_acc, values)
    return table - delta.astype(F32), new_lin, logits


def solution(mesh):
    in_specs = (
        P(None, "rows", "cols"),
        P(None, "rows", "cols", None),
        P(None, "rows"),
        P("cols", None, None),
        P("cols", None, None),
        P("cols", None),
        P("cols", None),
    )
    out_specs = (P("cols", None, None), P("cols", None), P(None, "rows"))
    return jax.shard_map(local, mesh=mesh, in_specs=in_specs, out_specs=out_specs, check_vma=False)
```
